512 devices in a mesh: strip: 128 (over y, z, core), grp: 4 (over x).
Axes of the slice: x: 4, y: 8, z: 8, core: 2. Of those that a mesh axis runs over, the one named last changes fastest.
Arguments:
- offsets: float32 [131072, 2, 128], P(('strip', 'grp')), may hold values from 0.5 to 14.5, as said below
- circulation: float32 [131072, 128], P(('strip', 'grp')), may hold values from -6 to 6
- window_anchor: float32 [131072, 2], P(('strip', 'grp')), may hold values from -8 to 8
- local_first: int32 [2, 131072], P(None, ('strip', 'grp')), may hold values from 0 to 255
- local_offset: int32 [2, 131072], P(None, ('strip', 'grp')), may hold values from 1 to 255
- cross_target: int32 [2, 131072], P(None, ('strip', 'grp')), may hold values from 0 to 255
- cross_source: int32 [2, 131072], P(None, ('strip', 'grp')), may hold values from 0 to 1023
- cross_count: int32 [2, 512], P(None, ('strip', 'grp')), may hold values from 16 to 256, as said below
- destination: int32 [2, 131072, 1], P(None, ('strip', 'grp')), may hold values from 0 to 127; in each aligned block of 256 rows (0 to 255, 256 to 511, ..., all dimensions but the last counted through in order) at most 2 rows name the same one
Outputs:
- final_circulation: float32 [131072, 128], P(('strip', 'grp'))
- final_anchor: float32 [131072, 2], P(('strip', 'grp'))
The draws below stay inside these ranges and needn't reach their ends.
Inputs may be any that keep to these rules, and one draw needn't show every extreme that they name: `offsets`: first component between 0.5 and 8 - 1.5, second between 0.5 and 16 - 1.5. `cross_count`: 256 on at least one device in each step. `destination`: in each step every device names each strip for exactly 2 of its leaves.
All inputs are finite; a program needn't handle non-finite values.
Results may differ from the reference program's by a relative error of at most 0.0003.
Values sent between devices are 32-bit elements; how exact they have to be, the bound alone decides.
A program may use at most 64 MiB of HBM per device.

```python
import math
import jax
import jax.numpy as jnp
import numpy as np
from jax import lax

LEAF_DEV = 256
WX = 8
WY = 16
STEPS = 2
P_SIZE = 128
LOCAL_DEV = 256
PAIR_DEV = 256
CAP = 2
LEAVES = 131072
N_STRIP = 128
N_GRP = 4


def draw_offsets(key, part):
    key = jax.random.fold_in(key, 11)
    key_x, key_y = jax.random.split(key)
    along_x = jax.random.uniform(key_x, (LEAVES, 1, P_SIZE), jnp.float32, 0.5, WX - 1.5)
    along_y = jax.random.uniform(key_y, (LEAVES, 1, P_SIZE), jnp.float32, 0.5, WY - 1.5)
    return jnp.concatenate([along_x, along_y], axis=1)


def draw_cross_count(key, part):
    key = jax.random.fold_in(key, 23)
    key_level, key_drop, key_top = jax.random.split(key, 3)
    count_shape = (STEPS, N_STRIP * N_GRP)
    levels = jax.random.randint(key_level, count_shape, 0, 4)
    base_count = jnp.right_shift(jnp.full(count_shape, PAIR_DEV, jnp.int32), levels)
    dropped = jax.random.randint(key_drop, count_shape, 0, base_count // 2 + 1)
    counts = base_count - dropped
    busiest = jax.random.randint(key_top, (STEPS, 1), 0, N_STRIP * N_GRP)
    columns = jnp.arange(N_STRIP * N_GRP, dtype=jnp.int32)[None, :]
    return jnp.where(columns == busiest, PAIR_DEV, counts).astype(jnp.int32)


def plant(array, own_key, least, high):
    longest = array.shape.index(max(array.shape))
    spots = []
    for shift in (0, 1):
        where = [jax.random.randint(jax.random.fold_in(own_key, axis), (), 0, length) for axis, length in enumerate(array.shape)]
        where[longest] = (where[longest] + shift) % array.shape[longest]
        spots.append(tuple(where))
    return array.at[spots[0]].set(least).at[spots[1]].set(high)


def steps_of(key, shape, cuts, low, high):
    def one(axis_at, shards_of):
        steps = jax.random.uniform(jax.random.fold_in(jax.random.fold_in(key, 6), axis_at), (shards_of,), jnp.float32, low / len(cuts), high / len(cuts))
        return jnp.repeat(jnp.exp(steps), shape[axis_at] // shards_of).reshape((-1,) + (1,) * (len(shape) - axis_at - 1))

    loudness = one(*cuts[0])
    for cut in cuts[1:]:
        loudness = loudness * one(*cut)
    return loudness


def assign_block(own_key, own, number, rows, amount, top, limit, skew):
    order = jax.random.permutation(own_key, amount)
    crowded, usual = portions_of(amount, rows * top, limit, skew, True), portions_of(amount, rows * top, limit, skew, False)
    places = jnp.arange(amount)

    def named(sizes, offset_by):
        used = int((sizes > 0).sum())
        fixed = max(1, used // 4)
        passed = fixed + (places - fixed + offset_by * (used - fixed)) % max(1, amount - fixed)
        return jnp.zeros((amount,), jnp.int32).at[order[jnp.where(places < fixed, places, passed)]].set(jnp.asarray(sizes, jnp.int32))

    sizes = jnp.where(number % 4 == 0, named(crowded, number // 4), named(usual, number - number // 4 - 1))
    mixed = jax.random.permutation(jax.random.fold_in(own, 3), amount)
    source_of, taker = mixed[0:amount // 2 * 2:2], mixed[1:amount // 2 * 2:2]
    margin = jnp.minimum(sizes[source_of] - 1, limit - sizes[taker]) // 2
    margin = jnp.where((source_of == order[0]) | (taker == order[0]) | (sizes[taker] == 0), 0, jnp.maximum(margin, 0))
    passed = jax.random.randint(jax.random.fold_in(own, 4), (amount // 2,), 0, 1 << 20) % (margin + 1)
    sizes = sizes.at[source_of].add(-passed).at[taker].add(passed)
    labels = jnp.searchsorted(jnp.cumsum(sizes), jnp.arange(rows * top), side="right").astype(jnp.int32)
    grid = labels.reshape(top, rows).T
    grid = grid[jax.random.permutation(jax.random.fold_in(own, 1), rows)]
    offset_by = jax.random.randint(jax.random.fold_in(own, 2), (rows, 1), 0, top)
    return jnp.take_along_axis(grid, (jnp.arange(top)[None, :] + offset_by) % top, axis=1)


def portions_of(count, total, bound, slope, full):
    weights = [(1 << 20) // math.isqrt(rank ** slope) + 1 for rank in range(1, count + 1)]
    largest = bound if full else min(bound, max(-(-total // count), total * weights[0] // sum(weights)))
    least = 1 if total - largest >= count - 1 else 0
    given, spare = [largest] + [least] * (count - 1), total - largest - least * (count - 1)
    while spare > 0:
        candidates = [i for i in range(1, count) if given[i] < largest] or [i for i in range(1, count) if given[i] < bound]
        mass, remaining = sum([weights[i] for i in candidates]), spare
        for i in candidates:
            extra = min(bound - given[i], max(1, remaining * weights[i] // mass), spare)
            given[i] = given[i] + extra
            spare = spare - extra
    return np.array(given)


def gaussian(key, extent, width, bound, cuts=(), kind=jnp.bfloat16):
    entries = jax.random.normal(key, extent, jnp.float32) * width
    if len(cuts) > 0:
        entries = steps_of(key, extent, cuts, -0.22, 0.18) * entries
    return jnp.clip(entries, min=-bound, max=bound).astype(kind)


def setup_inputs(seed: int = 0) -> dict:
    seeds = jax.random.split(jax.random.key(seed), 10)
    offsets = draw_offsets(jax.random.fold_in(seeds[9], 71), 0)
    circulation = gaussian(seeds[1], (LEAVES, P_SIZE), 1.0, 6.0, ((0, 512),), jnp.float32)
    window_anchor = jnp.clip(jax.random.uniform(seeds[2], (LEAVES, 2), jnp.float32, -8.0, 8.0) * steps_of(seeds[2], (LEAVES, 2), ((0, 512),), -0.4, 0.0), -8.0, 8.0)
    local_first = plant(jax.random.randint(seeds[3], (STEPS, N_STRIP * N_GRP * LOCAL_DEV), 0, LEAF_DEV), jax.random.fold_in(seeds[3], 1), 0, LEAF_DEV - 1).astype(jnp.int32)
    local_offset = plant(jax.random.randint(seeds[4], (STEPS, N_STRIP * N_GRP * LOCAL_DEV), 1, LEAF_DEV), jax.random.fold_in(seeds[4], 1), 1, LEAF_DEV - 1).astype(jnp.int32)
    cross_target = plant(jax.random.randint(seeds[5], (STEPS, N_STRIP * N_GRP * PAIR_DEV), 0, LEAF_DEV), jax.random.fold_in(seeds[5], 1), 0, LEAF_DEV - 1).astype(jnp.int32)
    cross_source = plant(jax.random.randint(seeds[6], (STEPS, N_STRIP * N_GRP * PAIR_DEV), 0, N_GRP * LEAF_DEV), jax.random.fold_in(seeds[6], 1), 0, (N_GRP * LEAF_DEV) - 1).astype(jnp.int32)
    cross_count = draw_cross_count(jax.random.fold_in(seeds[9], 71), 0)
    destination_keys = jax.random.split(jax.random.fold_in(seeds[8], 1), STEPS * LEAVES // LEAF_DEV)
    destination_turns = jax.random.permutation(jax.random.fold_in(seeds[8], 3), STEPS * LEAVES // LEAF_DEV)
    destination = jax.vmap(lambda own, number: assign_block(jax.random.fold_in(seeds[8], 2), own, number, LEAF_DEV, N_STRIP, 1, CAP, 0))(destination_keys, destination_turns).reshape((STEPS, LEAVES, 1))
    return {"offsets": offsets, "circulation": circulation, "window_anchor": window_anchor, "local_first": local_first, "local_offset": local_offset, "cross_target": cross_target, "cross_source": cross_source, "cross_count": cross_count, "destination": destination}


time_step = 0.5
smoothing = 1.0
biot_factor = 0.15915494309189535


def remesh_kernel(distance):
    radius = jnp.abs(distance)
    inner_part = 1.0 - 2.5 * radius * radius + 1.5 * radius * radius * radius
    outer_part = 0.5 * (2.0 - radius) * (2.0 - radius) * (1.0 - radius)
    return jnp.where(radius < 1.0, inner_part, jnp.where(radius < 2.0, outer_part, 0.0))


def one_sided(targets, sources):
    delta_x = targets[:, 0, :, None] - sources[:, 0, None, :]
    delta_y = targets[:, 1, :, None] - sources[:, 1, None, :]
    weight = biot_factor / (delta_x * delta_x + delta_y * delta_y + smoothing)
    source_gamma = sources[:, 2, None, :]
    along_x = -jnp.sum(source_gamma * delta_y * weight, axis=2)
    along_y = jnp.sum(source_gamma * delta_x * weight, axis=2)
    return jnp.stack([along_x, along_y], axis=1)


def mutual(targets, sources):
    delta_x = targets[:, 0, :, None] - sources[:, 0, None, :]
    delta_y = targets[:, 1, :, None] - sources[:, 1, None, :]
    weight = biot_factor / (delta_x * delta_x + delta_y * delta_y + smoothing)
    tilt_x = delta_x * weight
    tilt_y = delta_y * weight
    source_gamma = sources[:, 2, None, :]
    target_gamma = targets[:, 2, :, None]
    on_targets = jnp.stack([-jnp.sum(source_gamma * tilt_y, axis=2), jnp.sum(source_gamma * tilt_x, axis=2)], axis=1)
    on_sources = jnp.stack([jnp.sum(target_gamma * tilt_y, axis=1), -jnp.sum(target_gamma * tilt_x, axis=1)], axis=1)
    return on_targets, on_sources


def self_field(packed):
    leaf_total = packed.shape[0]

    def block_self(block_rows):
        return one_sided(block_rows, block_rows)

    blocks = lax.map(block_self, packed.reshape(-1, 128, 3, P_SIZE))
    return blocks.reshape(leaf_total, 2, P_SIZE)


def pair_field(packed, firsts, seconds, live_mask):
    def block_pairs(pieces):
        first_rows, second_rows, mask_rows = pieces
        on_first, on_second = mutual(packed[first_rows], packed[second_rows])
        return on_first * mask_rows[:, None, None], on_second * mask_rows[:, None, None]

    on_first, on_second = lax.map(block_pairs, (firsts.reshape(-1, 128), seconds.reshape(-1, 128), live_mask.reshape(-1, 128)))
    return on_first.reshape(-1, 2, P_SIZE), on_second.reshape(-1, 2, P_SIZE)


def remesh_leaves(advected, strength):
    axis_x = jnp.arange(WX, dtype=jnp.float32)
    axis_y = jnp.arange(WY, dtype=jnp.float32)

    def block_nodes(pieces):
        part_moved, part_gamma = pieces
        weight_x = remesh_kernel(part_moved[:, 0, None, :] - axis_x[None, :, None])
        weight_y = remesh_kernel(part_moved[:, 1, None, :] - axis_y[None, :, None])
        grid_nodes = jnp.einsum("lip,ljp->lij", weight_x * part_gamma[:, None, :], weight_y, precision=lax.Precision.HIGHEST)
        return grid_nodes.reshape(part_gamma.shape[0], WX * WY)

    leaf_total = strength.shape[0]
    blocks = lax.map(block_nodes, (advected.reshape(-1, 32, 2, P_SIZE), strength.reshape(-1, 32, P_SIZE)))
    return blocks.reshape(leaf_total, P_SIZE)


def reference(offsets, circulation, window_anchor, local_first, local_offset, cross_target, cross_source, cross_count, destination):
    devices = N_STRIP * N_GRP
    device_ids = jnp.arange(devices, dtype=jnp.int32)
    strip_ids = device_ids // N_GRP
    group_ids = device_ids % N_GRP
    leaf_base = (device_ids * LEAF_DEV)[:, None]
    upper_base = (((strip_ids + 1) % N_STRIP) * (N_GRP * LEAF_DEV))[:, None]
    particle_ids = jnp.arange(P_SIZE, dtype=jnp.int32)
    node_grid = jnp.stack([particle_ids // WY, particle_ids % WY]).astype(jnp.float32)
    anchor = window_anchor
    shifted = offsets
    strength = circulation
    for step_index in range(STEPS):
        position = anchor[:, :, None] + shifted
        packed = jnp.concatenate([position, strength[:, None, :]], axis=1)
        velocity = self_field(packed)
        local_rows = local_first[step_index].reshape(devices, LOCAL_DEV)
        local_steps = local_offset[step_index].reshape(devices, LOCAL_DEV)
        firsts = (leaf_base + local_rows).reshape(-1).astype(jnp.int32)
        partners = (leaf_base + (local_rows + local_steps) % LEAF_DEV).reshape(-1).astype(jnp.int32)
        ones_live = jnp.ones(firsts.shape, jnp.float32)
        on_first, on_second = pair_field(packed, firsts, partners, ones_live)
        velocity = velocity.at[firsts].add(on_first).at[partners].add(on_second)
        targets = (leaf_base + cross_target[step_index].reshape(devices, PAIR_DEV)).reshape(-1).astype(jnp.int32)
        sources = (upper_base + cross_source[step_index].reshape(devices, PAIR_DEV)).reshape(-1).astype(jnp.int32)
        live_mask = (jnp.arange(PAIR_DEV, dtype=jnp.int32)[None, :] < cross_count[step_index][:, None]).astype(jnp.float32).reshape(-1)
        on_targets, on_sources = pair_field(packed, targets, sources, live_mask)
        velocity = velocity.at[targets].add(on_targets).at[sources].add(on_sources)
        advected = shifted + time_step * velocity
        node_values = remesh_leaves(advected, strength)
        wanted = destination[step_index][:, 0].reshape(devices, LEAF_DEV)
        onehot = (wanted[:, :, None] == jnp.arange(N_STRIP, dtype=jnp.int32)[None, None, :]).astype(jnp.int32)
        earlier = (jnp.cumsum(onehot, axis=1) - onehot).astype(jnp.int32)
        within = jnp.sum(earlier * onehot, axis=2).astype(jnp.int32)
        new_index = ((wanted * N_GRP + group_ids[:, None]) * LEAF_DEV + strip_ids[:, None] * CAP + within).reshape(-1).astype(jnp.int32)
        strength = jnp.zeros_like(node_values).at[new_index].set(node_values)
        anchor = jnp.zeros_like(anchor).at[new_index].set(anchor)
        shifted = jnp.broadcast_to(node_grid[None], advected.shape)
    return strength, anchor
```

```python
import functools
import jax
import jax.numpy as jnp
import numpy as np
from jax import lax
from jax.experimental import pallas as pl
from jax.experimental.pallas import tpu as pltpu
from jax.sharding import PartitionSpec as P

WX = 8
WY = 16
STEPS = 2
time_step = 0.5
biot_factor = 0.15915494309189535
LANES = 128
f32 = jnp.float32
bf16 = jnp.bfloat16


def recip(x):
    return pl.reciprocal(x, approx=True)


def mutual_lanes(a_refs, b_refs, on_a, on_b):
    xa_ref, ya_ref, ga_ref = a_refs
    xb_ref, yb_ref, gb_ref = b_refs
    ua_ref, va_ref = on_a
    ub_ref, vb_ref = on_b
    ub_ref[...] = jnp.zeros_like(ub_ref)
    vb_ref[...] = jnp.zeros_like(vb_ref)
    zero = jnp.zeros((8, LANES), f32)

    def over_a(ia, carry):
        a0 = pl.multiple_of(ia * 8, 8)

        def over_b(ib, acc):
            acc = list(acc)
            rows = pl.ds(pl.multiple_of(ib * 8, 8), 8)
            xb, yb, gb = xb_ref[rows, :], yb_ref[rows, :], gb_ref[rows, :]
            ub, vb = ub_ref[rows, :], vb_ref[rows, :]
            for r in range(8):
                row = pl.ds(a0 + r, 1)
                dx = xa_ref[row, :] - xb
                dy = ya_ref[row, :] - yb
                w = recip(dx * dx + dy * dy + 1.0)
                tx = dx * w
                ty = dy * w
                acc[r] = acc[r] + gb * ty
                acc[8 + r] = acc[8 + r] + gb * tx
                ga = ga_ref[row, :]
                ub = ub + ga * ty
                vb = vb + ga * tx
            ub_ref[rows, :] = ub
            vb_ref[rows, :] = vb
            return tuple(acc)

        acc = lax.fori_loop(0, 16, over_b, (zero,) * 16)
        for r in range(8):
            ua_ref[pl.ds(a0 + r, 1), :] = jnp.sum(acc[r], axis=0, keepdims=True)
            va_ref[pl.ds(a0 + r, 1), :] = jnp.sum(acc[8 + r], axis=0, keepdims=True)
        return carry

    lax.fori_loop(0, 16, over_a, 0)


def self_lanes(a_refs, on_a):
    xa_ref, ya_ref, ga_ref = a_refs
    ua_ref, va_ref = on_a
    zero = jnp.zeros((8, LANES), f32)

    def over_a(ia, carry):
        a0 = pl.multiple_of(ia * 8, 8)

        def over_b(ib, acc):
            acc = list(acc)
            rows = pl.ds(pl.multiple_of(ib * 8, 8), 8)
            xb, yb, gb = xa_ref[rows, :], ya_ref[rows, :], ga_ref[rows, :]
            for r in range(8):
                row = pl.ds(a0 + r, 1)
                dx = xa_ref[row, :] - xb
                dy = ya_ref[row, :] - yb
                w = gb * recip(dx * dx + dy * dy + 1.0)
                acc[r] = acc[r] + dy * w
                acc[8 + r] = acc[8 + r] + dx * w
            return tuple(acc)

        acc = lax.fori_loop(0, 16, over_b, (zero,) * 16)
        for r in range(8):
            ua_ref[pl.ds(a0 + r, 1), :] = jnp.sum(acc[r], axis=0, keepdims=True)
            va_ref[pl.ds(a0 + r, 1), :] = jnp.sum(acc[8 + r], axis=0, keepdims=True)
        return carry

    lax.fori_loop(0, 16, over_a, 0)


def loop8(count, body):
    def eight(k, carry):
        for u in range(8):
            body(k * 8 + u)
        return carry

    lax.fori_loop(0, count // 8, eight, 0)


def rank_order(dest_ref, order_ref, count_ref, step):
    leaves = order_ref.shape[1]
    per_strip = 2

    def clear(k):
        count_ref[k] = 0

    def place(leaf):
        t = dest_ref[step, leaf]
        r = count_ref[t]
        count_ref[t] = r + 1
        order_ref[step, t * per_strip + r] = leaf

    loop8(leaves // per_strip, clear)
    loop8(leaves, place)


def local_kernel(state_ref, first_ref, second_ref, dest_ref, vel_ref, order_ref, ta, tb, ra, rb, oa, ob, count_ref):
    leaves = state_ref.shape[1]
    groups = leaves // LANES
    a_refs = [ta.at[c] for c in range(3)]
    b_refs = [tb.at[c] for c in range(3)]
    on_a = [oa.at[c] for c in range(2)]
    on_b = [ob.at[c] for c in range(2)]
    for step in range(STEPS):
        rank_order(dest_ref, order_ref, count_ref, step)

    def self_group(i, carry):
        rows = pl.ds(pl.multiple_of(i * LANES, LANES), LANES)
        for c in range(3):
            ta[c] = state_ref[c, rows, :].T
        self_lanes(a_refs, on_a)
        vel_ref[0, rows, :] = oa[0].T * -biot_factor
        vel_ref[1, rows, :] = oa[1].T * biot_factor
        return carry

    lax.fori_loop(0, groups, self_group, 0)

    def pair_group(i, carry):
        base = i * LANES

        def fetch(k):
            first = first_ref[base + k]
            second = second_ref[base + k]
            for c in range(3):
                ra[c, pl.ds(k, 1), :] = state_ref[c, pl.ds(first, 1), :]
                rb[c, pl.ds(k, 1), :] = state_ref[c, pl.ds(second, 1), :]

        loop8(LANES, fetch)
        for c in range(3):
            ta[c] = ra[c].T
            tb[c] = rb[c].T
        mutual_lanes(a_refs, b_refs, on_a, on_b)
        ra[0] = oa[0].T * -biot_factor
        ra[1] = oa[1].T * biot_factor
        rb[0] = ob[0].T * biot_factor
        rb[1] = ob[1].T * -biot_factor

        def spread(k):
            first = first_ref[base + k]
            second = second_ref[base + k]
            for c in range(2):
                vel_ref[c, pl.ds(first, 1), :] += ra[c, pl.ds(k, 1), :]
                vel_ref[c, pl.ds(second, 1), :] += rb[c, pl.ds(k, 1), :]

        loop8(LANES, spread)
        return carry

    lax.fori_loop(0, first_ref.shape[0] // LANES, pair_group, 0)


def cross_kernel(state_ref, far_ref, vel_in_ref, target_ref, source_ref, live_ref, vel_ref, part_ref, ta, tb, ra, rb, oa, ob):
    leaves = state_ref.shape[1]
    a_refs = [ta.at[c] for c in range(3)]
    b_refs = [tb.at[c] for c in range(3)]
    on_a = [oa.at[c] for c in range(2)]
    on_b = [ob.at[c] for c in range(2)]
    vel_ref[...] = vel_in_ref[...]
    part_ref[...] = jnp.zeros_like(part_ref)
    live = live_ref[0]

    def pair_group(i, carry):
        base = i * LANES

        def fetch(k):
            target = target_ref[base + k]
            source = source_ref[base + k]
            block = source // leaves
            row = source % leaves
            for c in range(3):
                ra[c, pl.ds(k, 1), :] = state_ref[c, pl.ds(target, 1), :]
                rb[c, pl.ds(k, 1), :] = far_ref[block, c, pl.ds(row, 1), :]

        loop8(LANES, fetch)
        for c in range(3):
            ta[c] = ra[c].T
            tb[c] = rb[c].T
        mutual_lanes(a_refs, b_refs, on_a, on_b)
        ra[0] = oa[0].T * -biot_factor
        ra[1] = oa[1].T * biot_factor
        rb[0] = ob[0].T * biot_factor
        rb[1] = ob[1].T * -biot_factor

        def spread(k, carry):
            target = target_ref[base + k]
            source = source_ref[base + k]
            block = source // leaves
            row = source % leaves
            for c in range(2):
                vel_ref[c, pl.ds(target, 1), :] += ra[c, pl.ds(k, 1), :]
                part_ref[block, c, pl.ds(row, 1), :] += rb[c, pl.ds(k, 1), :]
            return carry

        lax.fori_loop(0, jnp.minimum(live - base, LANES), spread, 0)
        return carry

    lax.fori_loop(0, (live + LANES - 1) // LANES, pair_group, 0)


def node_weight(distance):
    r = jnp.abs(distance)
    inner = 1.0 + r * r * (1.5 * r - 2.5)
    s = jnp.maximum(2.0 - r, 0.0)
    outer = (0.5 * s) * s * (1.0 - r)
    return jnp.where(r < 1.0, inner, outer)


def remesh_lanes(px_ref, py_ref, g_ref, wx_ref, nodes_ref):
    ix = lax.broadcasted_iota(jnp.int32, (WX, LANES), 0).astype(f32)
    iy = lax.broadcasted_iota(jnp.int32, (WX, LANES), 0).astype(f32)

    def over_p(p4, acc):
        acc = list(acc)
        for u in range(2):
            p = p4 * 2 + u
            row = pl.ds(p, 1)
            wx_ref[u] = node_weight(px_ref[row, :] - ix) * g_ref[row, :]
            y = py_ref[row, :] - iy
            wy = (node_weight(y), node_weight(y - 8.0))
            for i in range(WX):
                wxi = wx_ref[u, i : i + 1, :]
                for h in range(2):
                    acc[2 * i + h] = acc[2 * i + h] + wxi * wy[h]
        return tuple(acc)

    acc = lax.fori_loop(0, LANES // 2, over_p, (jnp.zeros((8, LANES), f32),) * 16)
    for i in range(16):
        nodes_ref[8 * i : 8 * i + 8, :] = acc[i]


def remesh_kernel(vel_ref, arrived_ref, shift_ref, g_ref, nodes_ref, px, py, pg, wx, out):
    leaves = g_ref.shape[0]
    blocks = arrived_ref.shape[0]

    def group(i, carry):
        rows = pl.ds(pl.multiple_of(i * LANES, LANES), LANES)
        for c, dst in ((0, px), (1, py)):
            total = vel_ref[c, rows, :]
            for b in range(blocks):
                total = total + arrived_ref[b, c, rows, :]
            dst[...] = (shift_ref[c, rows, :] + time_step * total).T
        pg[...] = g_ref[rows, :].T
        remesh_lanes(px, py, pg, wx, out)
        nodes_ref[rows, :] = out[...].T
        return carry

    lax.fori_loop(0, leaves // LANES, group, 0)


def split(x):
    hi = x.astype(bf16)
    return hi, (x - hi.astype(f32)).astype(bf16)


def dot3(x, m_hi, m_lo):
    hi, lo = split(x)
    d = functools.partial(jnp.dot, preferred_element_type=f32)
    return d(hi, m_hi) + (d(hi, m_lo) + d(lo, m_hi))


@functools.cache
def fourier_tables():
    n1, n2 = 2 * WX - 1, 2 * WY - 1
    size = n1 * n2
    u = np.arange(n1)
    v = np.arange(n2)
    di = np.where(u < WX, u, u - n1)
    dj = np.where(v < WY, v, v - n2)
    DI, DJ = [t.reshape(-1).astype(np.float64) for t in np.meshgrid(di, dj, indexing="ij")]
    k1, k2 = [t.reshape(-1) for t in np.meshgrid(u, v, indexing="ij")]
    keep = [0]
    for m in range(1, size):
        mirror = ((-k1[m]) % n1) * n2 + ((-k2[m]) % n2)
        if m < mirror:
            keep.append(m)
    f1, f2 = k1[keep].astype(np.float64), k2[keep].astype(np.float64)
    nf = len(keep)

    def phase(i, j):
        return 2 * np.pi * (np.outer(i, f1) / n1 + np.outer(j, f2) / n2)

    forward = np.zeros((512, 512))
    p = phase(DI, DJ)
    forward[:size, :nf] = np.cos(p)
    forward[:size, 256 : 256 + nf] = -np.sin(p)
    node = np.arange(WX * WY)
    q = phase(node // WY, node % WY)
    gamma = np.zeros((128, 512))
    gamma[:, :nf] = np.cos(q)
    gamma[:, 256 : 256 + nf] = -np.sin(q)
    weight = np.full(nf, 2.0 / size)
    weight[0] = 1.0 / size
    inverse = np.zeros((512, 128))
    inverse[:nf] = weight[:, None] * np.cos(q).T
    inverse[256 : 256 + nf] = -weight[:, None] * np.sin(q).T
    lattice = np.zeros((8, 512))
    lattice[0, :size] = DI
    lattice[1, :size] = DJ
    ddx = (node // WY)[:, None] - (node // WY)[None, :]
    ddy = (node % WY)[:, None] - (node % WY)[None, :]
    w = biot_factor / (ddx * ddx + ddy * ddy + 1.0)
    own = np.concatenate([(-ddy * w).T, (ddx * w).T], axis=1)

    def halves(x):
        hi = x.astype(np.float32).astype(bf16)
        lo = (x - hi.astype(np.float64)).astype(np.float32).astype(bf16)
        return np.stack([hi, lo])

    return halves(forward), halves(gamma), halves(inverse), lattice.astype(np.float32), halves(own)


def pair_waves(ga, gb, gap, fwd, gam, inv, lat):
    x = gap[:, 0:1] + lat[0:1, :]
    y = gap[:, 64:65] + lat[1:2, :]
    w = biot_factor * recip(x * x + y * y + 1.0)
    kx = dot3(-y * w, fwd[0], fwd[1])
    ky = dot3(x * w, fwd[0], fwd[1])
    wa = dot3(ga, gam[0], gam[1])
    wb = dot3(gb, gam[0], gam[1])
    ar, ai = wa[:, :256], wa[:, 256:]
    br, bi = wb[:, :256], wb[:, 256:]
    on_a, on_b = [], []
    for k in (kx, ky):
        kr, ki = k[:, :256], k[:, 256:]
        on_a.append(dot3(jnp.concatenate([kr * br - ki * bi, kr * bi + ki * br], axis=1), inv[0], inv[1]))
        on_b.append(dot3(jnp.concatenate([kr * ar + ki * ai, kr * ai - ki * ar], axis=1), inv[0], inv[1]))
    return on_a, on_b


def local_waves(g_ref, anc_ref, first_ref, second_ref, fwd_ref, gam_ref, inv_ref, lat_ref, own_ref, vel_ref, ra, rb, rd):
    own = dot3(g_ref[...], own_ref[0], own_ref[1])
    vel_ref[0] = own[:, :128]
    vel_ref[1] = own[:, 128:]
    rows = ra.shape[1]

    def pair_group(i, carry):
        base = i * rows

        def fetch(k):
            first = pl.ds(first_ref[base + k], 1)
            second = pl.ds(second_ref[base + k], 1)
            row = pl.ds(k, 1)
            ra[0, row, :] = g_ref[first, :]
            rb[0, row, :] = g_ref[second, :]
            rd[row, :] = anc_ref[first, :] - anc_ref[second, :]

        loop8(rows, fetch)
        on_a, on_b = pair_waves(ra[0], rb[0], rd[...], fwd_ref, gam_ref, inv_ref, lat_ref)
        for c in range(2):
            ra[c] = on_a[c]
            rb[c] = on_b[c]

        def spread(k):
            first = pl.ds(first_ref[base + k], 1)
            second = pl.ds(second_ref[base + k], 1)
            for c in range(2):
                vel_ref[c, first, :] += ra[c, pl.ds(k, 1), :]
                vel_ref[c, second, :] -= rb[c, pl.ds(k, 1), :]

        loop8(rows, spread)
        return carry

    lax.fori_loop(0, first_ref.shape[0] // rows, pair_group, 0)


def cross_waves(g_ref, anc_ref, far_ref, vel_in_ref, target_ref, source_ref, live_ref, fwd_ref, gam_ref, inv_ref, lat_ref, vel_ref, part_ref, ra, rb, rd):
    leaves = g_ref.shape[0]
    rows = ra.shape[1]
    vel_ref[...] = vel_in_ref[...]
    part_ref[...] = jnp.zeros_like(part_ref)
    live = live_ref[0]

    def pair_group(i, carry):
        base = i * rows

        def fetch(k):
            target = pl.ds(target_ref[base + k], 1)
            source = source_ref[base + k]
            block = source // leaves
            other = pl.ds(source % leaves, 1)
            row = pl.ds(k, 1)
            ra[0, row, :] = g_ref[target, :]
            rb[0, row, :] = far_ref[block, 0, other, :]
            rd[row, :] = anc_ref[target, :] - far_ref[block, 1, other, :]

        loop8(rows, fetch)
        on_a, on_b = pair_waves(ra[0], rb[0], rd[...], fwd_ref, gam_ref, inv_ref, lat_ref)
        for c in range(2):
            ra[c] = on_a[c]
            rb[c] = on_b[c]

        def spread(k, carry):
            target = pl.ds(target_ref[base + k], 1)
            source = source_ref[base + k]
            block = source // leaves
            other = pl.ds(source % leaves, 1)
            for c in range(2):
                vel_ref[c, target, :] += ra[c, pl.ds(k, 1), :]
                part_ref[block, c, other, :] -= rb[c, pl.ds(k, 1), :]
            return carry

        lax.fori_loop(0, jnp.minimum(live - base, rows), spread, 0)
        return carry

    lax.fori_loop(0, (live + rows - 1) // rows, pair_group, 0)


def vspec():
    return pl.BlockSpec(memory_space=pltpu.VMEM)


def sspec():
    return pl.BlockSpec(memory_space=pltpu.SMEM)


def tile():
    return pltpu.VMEM((LANES, LANES), f32)


def tiles(n):
    return pltpu.VMEM((n, LANES, LANES), f32)


def call(kernel, out_shape, in_specs, out_specs, scratch, flops=1e9, **kw):
    return pl.pallas_call(
        kernel,
        out_shape=out_shape,
        in_specs=in_specs,
        out_specs=out_specs,
        scratch_shapes=scratch,
        compiler_params=pltpu.CompilerParams(vmem_limit_bytes=40 * 2**20, **kw),
        cost_estimate=pl.CostEstimate(flops=int(flops), bytes_accessed=2**21, transcendentals=0),
    )


def run_local(state, first, second, dest):
    leaves = state.shape[1]
    return call(
        local_kernel,
        (jax.ShapeDtypeStruct((2, leaves, LANES), f32), jax.ShapeDtypeStruct((STEPS, leaves), jnp.int32)),
        [vspec(), sspec(), sspec(), sspec()],
        (vspec(), sspec()),
        [tiles(3), tiles(3), tiles(3), tiles(3), tiles(2), tiles(2), pltpu.SMEM((leaves // 2,), jnp.int32)],
        flops=3e9,
    )(state, first, second, dest)


def run_cross(state, far, vel, target, source, live):
    leaves = state.shape[1]
    return call(
        cross_kernel,
        (jax.ShapeDtypeStruct(vel.shape, f32), jax.ShapeDtypeStruct((far.shape[0], 2, leaves, LANES), f32)),
        [vspec(), vspec(), vspec(), sspec(), sspec(), sspec()],
        (vspec(), vspec()),
        [tiles(3), tiles(3), tiles(3), tiles(3), tiles(2), tiles(2)],
    )(state, far, vel, target, source, live)


def run_remesh(vel, arrived, shifted, strength):
    return call(
        remesh_kernel,
        jax.ShapeDtypeStruct(strength.shape, f32),
        [vspec()] * 4,
        vspec(),
        [tile(), tile(), tile(), pltpu.VMEM((2, WX, LANES), f32), tile()],
    )(vel, arrived, shifted, strength)


def run_local_waves(strength, anc, first, second, tables, rows=128):
    leaves = strength.shape[0]
    fwd, gam, inv, lat, own = tables
    return call(
        local_waves,
        jax.ShapeDtypeStruct((2, leaves, LANES), f32),
        [vspec(), vspec(), sspec(), sspec()] + [vspec()] * 5,
        vspec(),
        [pltpu.VMEM((2, rows, LANES), f32), pltpu.VMEM((2, rows, LANES), f32), pltpu.VMEM((rows, LANES), f32)],
    )(strength, anc, first, second, fwd, gam, inv, lat, own)


def run_cross_waves(strength, anc, far, vel, target, source, live, tables, rows=128):
    leaves = strength.shape[0]
    fwd, gam, inv, lat, own = tables
    return call(
        cross_waves,
        (jax.ShapeDtypeStruct(vel.shape, f32), jax.ShapeDtypeStruct((far.shape[0], 2, leaves, LANES), f32)),
        [vspec()] * 4 + [sspec()] * 3 + [vspec()] * 4,
        (vspec(), vspec()),
        [pltpu.VMEM((2, rows, LANES), f32), pltpu.VMEM((2, rows, LANES), f32), pltpu.VMEM((rows, LANES), f32)],
    )(strength, anc, far, vel, target, source, live, fwd, gam, inv, lat)


def push_kernel(shift, block_ref, out_ref, send_sem, recv_sem):
    strip, grp = lax.axis_index("strip"), lax.axis_index("grp")
    strips, groups = lax.axis_size("strip"), lax.axis_size("grp")
    to = lax.rem(strip + shift + strips, strips)
    back = lax.rem(strip - shift + strips, strips)
    barrier = pltpu.get_barrier_semaphore()
    for j in range(groups):
        pl.semaphore_signal(barrier, inc=1, device_id={"strip": back, "grp": j})
    pl.semaphore_wait(barrier, groups)
    copies = []
    for j in range(groups):
        peer = lax.rem(grp + j, groups)
        copies.append(
            pltpu.make_async_remote_copy(
                src_ref=block_ref.at[peer] if shift > 0 else block_ref,
                dst_ref=out_ref.at[grp],
                send_sem=send_sem.at[j],
                recv_sem=recv_sem.at[j],
                device_id={"strip": to, "grp": peer},
            )
        )
    for copy in copies:
        copy.start()
    for copy in copies:
        copy.wait()


def push(block, shift, collective_id):
    groups = lax.axis_size("grp")
    shape = block.shape if shift > 0 else (groups,) + block.shape
    return pl.pallas_call(
        functools.partial(push_kernel, shift),
        out_shape=jax.ShapeDtypeStruct(shape, f32),
        in_specs=[pl.BlockSpec(memory_space=pl.ANY)],
        out_specs=pl.BlockSpec(memory_space=pl.ANY),
        scratch_shapes=[pltpu.SemaphoreType.DMA((groups,)), pltpu.SemaphoreType.DMA((groups,))],
        compiler_params=pltpu.CompilerParams(collective_id=collective_id, has_side_effects=True),
    )(block)


def regroup_kernel(step, nodes_ref, anchor_ref, order_ref, out_ref, outbox, send_sem, recv_sem, own_sem):
    strip = lax.axis_index("strip")
    strips = outbox.shape[0]
    barrier = pltpu.get_barrier_semaphore()

    def greet(d, carry):
        pl.semaphore_signal(barrier, inc=1, device_id={"strip": lax.rem(strip + d, strips)})
        return carry

    lax.fori_loop(1, strips, greet, 0)

    def fill(t, carry):
        for r in range(2):
            leaf = pl.ds(order_ref[step, 2 * t + r], 1)
            outbox[t, r : r + 1, :] = nodes_ref[leaf, :]
            outbox[t, 2 + r : 3 + r, :] = anchor_ref[leaf, :]
        return carry

    lax.fori_loop(0, strips, fill, 0)
    pl.semaphore_wait(barrier, strips - 1)

    def send(d, carry):
        to = lax.rem(strip + d, strips)
        pltpu.make_async_remote_copy(
            src_ref=outbox.at[to],
            dst_ref=out_ref.at[strip],
            send_sem=send_sem,
            recv_sem=recv_sem,
            device_id={"strip": to},
        ).start()
        return carry

    lax.fori_loop(1, strips, send, 0)
    own = pltpu.make_async_copy(outbox.at[strip], out_ref.at[strip], own_sem)
    own.start()
    own.wait()
    rest = pl.ds(0, strips - 1)
    pltpu.make_async_copy(outbox.at[rest], outbox.at[rest], send_sem).wait()
    pltpu.make_async_copy(out_ref.at[rest], out_ref.at[rest], recv_sem).wait()


def regroup(nodes, anchor, order, step, collective_id):
    strips = lax.axis_size("strip")
    shape = (strips, 4, LANES)
    return pl.pallas_call(
        functools.partial(regroup_kernel, step),
        out_shape=jax.ShapeDtypeStruct(shape, f32),
        in_specs=[vspec(), vspec(), sspec()],
        out_specs=vspec(),
        scratch_shapes=[pltpu.VMEM(shape, f32)] + [pltpu.SemaphoreType.DMA] * 3,
        compiler_params=pltpu.CompilerParams(
            collective_id=collective_id, has_side_effects=True, vmem_limit_bytes=16 * 2**20
        ),
    )(nodes, anchor, order)


def on_device(
    offsets,
    circulation,
    window_anchor,
    local_first,
    local_offset,
    cross_target,
    cross_source,
    cross_count,
    destination,
):
    leaves = circulation.shape[0]
    per_strip = leaves // lax.axis_size("strip")
    half = LANES // 2
    second = (local_first + local_offset) % leaves
    shifted = offsets.transpose(1, 0, 2)
    state = jnp.concatenate([shifted + window_anchor.T[:, :, None], circulation[None]], axis=0)
    anchor = jnp.repeat(window_anchor, half, axis=1)
    tables = [jnp.asarray(t) for t in fourier_tables()]
    far = push(state, -1, 0)
    vel, order = run_local(state, local_first[0], second[0], destination[:, :, 0])
    vel, part = run_cross(state, far, vel, cross_target[0], cross_source[0], cross_count[0])
    arrived = push(part, 1, 1)
    nodes = run_remesh(vel, arrived, shifted, circulation)
    box = regroup(nodes, anchor, order, 0, 2)
    strength = box[:, :per_strip].reshape(leaves, LANES)
    anchor = box[:, per_strip:].reshape(leaves, LANES)
    far = push(jnp.stack([strength, anchor]), -1, 3)
    vel = run_local_waves(strength, anchor, local_first[1], second[1], tables)
    vel, part = run_cross_waves(
        strength, anchor, far, vel, cross_target[1], cross_source[1], cross_count[1], tables
    )
    arrived = push(part, 1, 4)
    node = jnp.arange(LANES, dtype=jnp.int32)
    grid = jnp.stack([node // WY, node % WY]).astype(f32)
    shifted = jnp.broadcast_to(grid[:, None, :], vel.shape)
    nodes = run_remesh(vel, arrived, shifted, strength)
    box = regroup(nodes, anchor, order, 1, 5)
    strength = box[:, :per_strip].reshape(leaves, LANES)
    anchor = box[:, per_strip:, ::half].reshape(leaves, 2)
    return strength, anchor


def solution(mesh):
    rows = P(("strip", "grp"))
    lists = P(None, ("strip", "grp"))
    return jax.shard_map(
        on_device,
        mesh=mesh,
        in_specs=(rows, rows, rows, lists, lists, lists, lists, lists, lists),
        out_specs=(rows, rows),
        check_vma=False,
    )
```

```python
import functools
import jax
import jax.numpy as jnp
import numpy as np
from jax import lax
from jax.experimental import pallas as pl
from jax.experimental.pallas import tpu as pltpu
from jax.sharding import PartitionSpec as P

WX = 8
WY = 16
STEPS = 2
time_step = 0.5
biot_factor = 0.15915494309189535
LANES = 128
f32 = jnp.float32
bf16 = jnp.bfloat16


def recip(x):
    return pl.reciprocal(x, approx=True)


def mutual_lanes(a_refs, b_refs, on_a, on_b):
    xa_ref, ya_ref, ga_ref = a_refs
    xb_ref, yb_ref, gb_ref = b_refs
    ua_ref, va_ref = on_a
    ub_ref, vb_ref = on_b
    ub_ref[...] = jnp.zeros_like(ub_ref)
    vb_ref[...] = jnp.zeros_like(vb_ref)
    zero = jnp.zeros((8, LANES), f32)

    def over_a(ia, carry):
        a0 = pl.multiple_of(ia * 8, 8)

        def over_b(ib, acc):
            acc = list(acc)
            rows = pl.ds(pl.multiple_of(ib * 8, 8), 8)
            xb, yb, gb = xb_ref[rows, :], yb_ref[rows, :], gb_ref[rows, :]
            ub, vb = ub_ref[rows, :], vb_ref[rows, :]
            for r in range(8):
                row = pl.ds(a0 + r, 1)
                dx = xa_ref[row, :] - xb
                dy = ya_ref[row, :] - yb
                w = recip(dx * dx + dy * dy + 1.0)
                tx = dx * w
                ty = dy * w
                acc[r] = acc[r] + gb * ty
                acc[8 + r] = acc[8 + r] + gb * tx
                ga = ga_ref[row, :]
                ub = ub + ga * ty
                vb = vb + ga * tx
            ub_ref[rows, :] = ub
            vb_ref[rows, :] = vb
            return tuple(acc)

        acc = lax.fori_loop(0, 16, over_b, (zero,) * 16, unroll=8)
        for r in range(8):
            ua_ref[pl.ds(a0 + r, 1), :] = jnp.sum(acc[r], axis=0, keepdims=True)
            va_ref[pl.ds(a0 + r, 1), :] = jnp.sum(acc[8 + r], axis=0, keepdims=True)
        return carry

    lax.fori_loop(0, 16, over_a, 0)


def loop8(count, body):
    def eight(k, carry):
        for u in range(8):
            body(k * 8 + u)
        return carry

    lax.fori_loop(0, count // 8, eight, 0)


def node_weight(distance):
    r = jnp.abs(distance)
    inner = 1.0 + r * r * (1.5 * r - 2.5)
    s = jnp.maximum(2.0 - r, 0.0)
    outer = (0.5 * s) * s * (1.0 - r)
    return jnp.where(r < 1.0, inner, outer)


def remesh_lanes(px_ref, py_ref, g_ref, wx_ref, nodes_ref):
    ix = lax.broadcasted_iota(jnp.int32, (WX, LANES), 0).astype(f32)
    iy = lax.broadcasted_iota(jnp.int32, (WX, LANES), 0).astype(f32)

    def over_p(p4, acc):
        acc = list(acc)
        for u in range(2):
            p = p4 * 2 + u
            row = pl.ds(p, 1)
            wx_ref[u] = node_weight(px_ref[row, :] - ix) * g_ref[row, :]
            y = py_ref[row, :] - iy
            wy = (node_weight(y), node_weight(y - 8.0))
            for i in range(WX):
                wxi = wx_ref[u, i : i + 1, :]
                for h in range(2):
                    acc[2 * i + h] = acc[2 * i + h] + wxi * wy[h]
        return tuple(acc)

    acc = lax.fori_loop(0, LANES // 2, over_p, (jnp.zeros((8, LANES), f32),) * 16)
    for i in range(16):
        nodes_ref[8 * i : 8 * i + 8, :] = acc[i]


def split(x):
    hi = x.astype(bf16)
    return hi, (x - hi.astype(f32)).astype(bf16)


def dot3(x, m_hi, m_lo):
    hi, lo = split(x)
    d = functools.partial(jnp.dot, preferred_element_type=f32)
    return d(hi, m_hi) + (d(hi, m_lo) + d(lo, m_hi))


@functools.cache
def fourier_tables():
    n1, n2 = 2 * WX - 1, 2 * WY - 1
    size = n1 * n2
    u = np.arange(n1)
    v = np.arange(n2)
    di = np.where(u < WX, u, u - n1)
    dj = np.where(v < WY, v, v - n2)
    DI, DJ = [t.reshape(-1).astype(np.float64) for t in np.meshgrid(di, dj, indexing="ij")]
    k1, k2 = [t.reshape(-1) for t in np.meshgrid(u, v, indexing="ij")]
    keep = [0]
    for m in range(1, size):
        mirror = ((-k1[m]) % n1) * n2 + ((-k2[m]) % n2)
        if m < mirror:
            keep.append(m)
    f1, f2 = k1[keep].astype(np.float64), k2[keep].astype(np.float64)
    nf = len(keep)

    def phase(i, j):
        return 2 * np.pi * (np.outer(i, f1) / n1 + np.outer(j, f2) / n2)

    forward = np.zeros((512, 512))
    p = phase(DI, DJ)
    forward[:size, :nf] = np.cos(p)
    forward[:size, 256 : 256 + nf] = -np.sin(p)
    node = np.arange(WX * WY)
    q = phase(node // WY, node % WY)
    gamma = np.zeros((128, 512))
    gamma[:, :nf] = np.cos(q)
    gamma[:, 256 : 256 + nf] = -np.sin(q)
    weight = np.full(nf, 2.0 / size)
    weight[0] = 1.0 / size
    inverse = np.zeros((512, 128))
    inverse[:nf] = weight[:, None] * np.cos(q).T
    inverse[256 : 256 + nf] = -weight[:, None] * np.sin(q).T
    lattice = np.zeros((8, 512))
    lattice[0, :size] = DI
    lattice[1, :size] = DJ
    ddx = (node // WY)[:, None] - (node // WY)[None, :]
    ddy = (node % WY)[:, None] - (node % WY)[None, :]
    w = biot_factor / (ddx * ddx + ddy * ddy + 1.0)
    own = np.concatenate([(-ddy * w).T, (ddx * w).T], axis=1)

    def halves(x):
        hi = x.astype(np.float32).astype(bf16)
        lo = (x - hi.astype(np.float64)).astype(np.float32).astype(bf16)
        return np.stack([hi, lo])

    return halves(forward), halves(gamma), halves(inverse), lattice.astype(np.float32), halves(own)


def vspec():
    return pl.BlockSpec(memory_space=pltpu.VMEM)


def sspec():
    return pl.BlockSpec(memory_space=pltpu.SMEM)


def tile():
    return pltpu.VMEM((LANES, LANES), f32)


def tiles(n):
    return pltpu.VMEM((n, LANES, LANES), f32)


def one_sided_lanes(a_refs, b_refs, on_a):
    xa_ref, ya_ref = a_refs
    xb_ref, yb_ref, gb_ref = b_refs
    ua_ref, va_ref = on_a
    zero = jnp.zeros((8, LANES), f32)

    def over_a(ia, carry):
        a0 = pl.multiple_of(ia * 8, 8)

        def over_b(ib, acc):
            acc = list(acc)
            rows = pl.ds(pl.multiple_of(ib * 8, 8), 8)
            xb, yb, gb = xb_ref[rows, :], yb_ref[rows, :], gb_ref[rows, :]
            for r in range(8):
                row = pl.ds(a0 + r, 1)
                dx = xa_ref[row, :] - xb
                dy = ya_ref[row, :] - yb
                w = gb * recip(dx * dx + (dy * dy + 1.0))
                acc[r] = acc[r] + dy * w
                acc[8 + r] = acc[8 + r] + dx * w
            return tuple(acc)

        acc = lax.fori_loop(0, 16, over_b, (zero,) * 16, unroll=8)
        for r in range(8):
            ua_ref[pl.ds(a0 + r, 1), :] = jnp.sum(acc[r], axis=0, keepdims=True)
            va_ref[pl.ds(a0 + r, 1), :] = jnp.sum(acc[8 + r], axis=0, keepdims=True)
        return carry

    lax.fori_loop(0, 16, over_a, 0)


def dot(a, b):
    return jnp.dot(a, b, preferred_element_type=f32)


def onehot(condition):
    return jnp.where(condition, 1.0, 0.0).astype(bf16)


def dot_exact(hot, x):
    hi, rest = split(x)[0], None
    rest = x - hi.astype(f32)
    mid, lo = split(rest)
    return (dot(hot, hi) + dot(hot, mid)) + dot(hot, lo)


def dot_near(hot, x):
    hi, lo = split(x)
    return dot(hot, hi) + dot(hot, lo)


def spread_rows(index_row, x):
    leaves = index_row.shape[1]
    places = lax.broadcasted_iota(jnp.int32, (leaves, leaves), 0)
    return dot_near(onehot(places == index_row), x)


def earlier(n):
    return onehot(lax.broadcasted_iota(jnp.int32, (n, n), 0) < lax.broadcasted_iota(jnp.int32, (n, n), 1))


def sort_lists(target_ref, source_ref, live_ref, outbox):
    groups = outbox.shape[0]
    n = target_ref.shape[1]
    before = earlier(n)
    rows8 = lax.broadcasted_iota(jnp.int32, (8, n), 0)
    places = lax.broadcasted_iota(jnp.int32, (n, n), 0)
    k = lax.broadcasted_iota(jnp.int32, (1, n), 1)
    outbox[...] = jnp.zeros_like(outbox)
    for step in range(STEPS):
        source = source_ref[step : step + 1, :]
        owner = lax.shift_right_logical(source, n.bit_length() - 1)
        key = jnp.where(k < live_ref[step, 0], owner, groups)
        row = jnp.bitwise_and(source, n - 1)
        mine = jnp.where(rows8 == key, 1.0, 0.0)
        place = jnp.sum(mine * dot(mine.astype(bf16), before), axis=0, keepdims=True).astype(jnp.int32)
        values = jnp.where(rows8 == 0, target_ref[step : step + 1, :], jnp.where(rows8 == 1, row, 0))
        values = values.astype(f32).astype(bf16)
        count = jnp.sum(mine, axis=1, keepdims=True).astype(jnp.int32)
        for b in range(groups):
            hot = onehot((places == place) & (key == b))
            found = lax.dot_general(values, hot, (((1,), (1,)), ((), ())), preferred_element_type=f32)
            outbox[b, 2 * step : 2 * step + 2, :] = found[0:2, :].astype(jnp.int32)
            outbox[b, 4 + step : 5 + step, :] = jnp.broadcast_to(count[b : b + 1, :], (1, n))


class Ring:
    def __init__(self, block, own, up, down, halves, send_sem, recv_sem):
        self.block, self.own, self.up, self.down = block, own, up, down
        self.halves, self.send_sem, self.recv_sem = halves, send_sem, recv_sem
        self.grp = lax.axis_index("grp")
        groups = lax.axis_size("grp")
        self.right = lax.rem(self.grp + 1, groups)
        self.left = lax.rem(self.grp + groups - 1, groups)
        self.across = lax.rem(self.grp + 2, groups)
        strip, strips = lax.axis_index("strip"), lax.axis_size("strip")
        self.above = lax.rem(strip + 1, strips)
        self.below = lax.rem(strip + strips - 1, strips)
        self.sent = []

    def send(self, src, dst, device, slot):
        copy = pltpu.make_async_remote_copy(
            src_ref=src,
            dst_ref=dst,
            send_sem=self.send_sem.at[slot],
            recv_sem=self.recv_sem.at[slot],
            device_id=device,
        )
        copy.start()
        self.sent.append(copy)
        return copy

    def to_strips(self, src, member, slot):
        return [
            self.send(src, self.down.at[member], {"strip": self.above}, slot),
            self.send(src, self.up.at[member], {"strip": self.below}, slot + 1),
        ]

    def first(self):
        self.from_left = self.send(self.block, self.own.at[self.grp], {"grp": self.right}, 0)
        self.from_right = self.send(self.block, self.own.at[self.grp], {"grp": self.left}, 1)
        self.last = self.to_strips(self.block, self.grp, 2)

    def second(self):
        self.from_left.wait_recv()
        half = self.halves(self.own, self.left)[0]
        self.half_a = self.send(half, half, {"grp": self.right}, 4)
        self.last += self.to_strips(self.own.at[self.left], self.left, 5)
        self.from_right.wait_recv()
        half = self.halves(self.own, self.right)[1]
        self.half_b = self.send(half, half, {"grp": self.left}, 7)
        self.last += self.to_strips(self.own.at[self.right], self.right, 8)

    def third(self):
        self.half_a.wait_recv()
        self.half_b.wait_recv()
        self.last += self.to_strips(self.own.at[self.across], self.across, 10)

    def finish(self):
        for copy in self.last:
            copy.wait_recv()
        for copy in self.sent:
            copy.wait_send()


def local_kernel(
    block_ref,
    state_ref,
    first_ref,
    second_ref,
    first_row_ref,
    second_row_ref,
    target_ref,
    source_ref,
    live_ref,
    vel_ref,
    lists_ref,
    up_ref,
    down_ref,
    own_ref,
    outbox,
    ta,
    tb,
    oa,
    ob,
    ra,
    rb,
    send_sem,
    recv_sem,
    list_send,
    list_recv,
):
    leaves = state_ref.shape[1]
    halves = lambda own, member: [own.at[member, :, pl.ds(h * leaves // 2, leaves // 2)] for h in range(2)]
    ring = Ring(block_ref, own_ref, up_ref, down_ref, halves, send_sem, recv_sem)
    groups = lists_ref.shape[0]
    barrier = pltpu.get_barrier_semaphore()
    for device in ({"grp": ring.left}, {"grp": ring.right}, {"strip": ring.above}):
        pl.semaphore_signal(barrier, inc=1, device_id=device)
    for j in range(groups):
        pl.semaphore_signal(barrier, inc=1, device_id={"strip": ring.below, "grp": j})
    sort_lists(target_ref, source_ref, live_ref, outbox)
    pl.semaphore_wait(barrier, 3 + groups)
    ring.first()
    mail = []
    for j in range(groups):
        peer = lax.rem(ring.grp + j, groups)
        copy = pltpu.make_async_remote_copy(
            src_ref=outbox.at[peer],
            dst_ref=lists_ref.at[ring.grp],
            send_sem=list_send.at[j],
            recv_sem=list_recv.at[j],
            device_id={"strip": ring.above, "grp": peer},
        )
        copy.start()
        mail.append(copy)

    def self_group(i, carry):
        rows = pl.ds(pl.multiple_of(i * LANES, LANES), LANES)
        for c in range(3):
            ta[c] = state_ref[c, rows, :].T
        one_sided_lanes((ta.at[0], ta.at[1]), (ta.at[0], ta.at[1], ta.at[2]), (oa.at[0], oa.at[1]))
        vel_ref[0, rows, :] = oa[0].T * -biot_factor
        vel_ref[1, rows, :] = oa[1].T * biot_factor
        return carry

    def pair_group(i):
        base = i * LANES
        rows = pl.ds(base, LANES)

        def fetch(k):
            first = first_ref[base + k]
            second = second_ref[base + k]
            for c in range(3):
                ra[c, pl.ds(base + k, 1), :] = state_ref[c, pl.ds(first, 1), :]
                rb[c, pl.ds(base + k, 1), :] = state_ref[c, pl.ds(second, 1), :]

        loop8(LANES, fetch)
        for c in range(3):
            ta[c] = ra[c, rows, :].T
            tb[c] = rb[c, rows, :].T
        mutual_lanes(
            [ta.at[c] for c in range(3)],
            [tb.at[c] for c in range(3)],
            [oa.at[c] for c in range(2)],
            [ob.at[c] for c in range(2)],
        )
        ra[0, rows, :] = oa[0].T * -biot_factor
        ra[1, rows, :] = oa[1].T * biot_factor
        rb[0, rows, :] = ob[0].T * biot_factor
        rb[1, rows, :] = ob[1].T * -biot_factor

    lax.fori_loop(0, leaves // LANES, self_group, 0)
    ring.second()
    pair_group(0)
    ring.third()
    for i in range(1, leaves // LANES):
        pair_group(i)
    for c in range(2):
        vel_ref[c] += spread_rows(first_row_ref[...], ra[c]) + spread_rows(second_row_ref[...], rb[c])
    ring.finish()
    for copy in mail:
        copy.wait()


def walk(target_ref, source_ref, live_ref, lists_ref, leaves, step, visit):
    live = live_ref[step, 0]

    def mine(k, carry):
        source = source_ref[step, k]
        visit(k, target_ref[step, k], 0, source // leaves, source % leaves)
        return carry

    lax.fori_loop(0, live, mine, 0)
    base = live
    for g in range(lists_ref.shape[0]):
        count = lists_ref[g, 4 + step, 0]

        def theirs(k, carry, g=g, base=base):
            visit(base + k, lists_ref[g, 2 * step + 1, k], 1, g, lists_ref[g, 2 * step, k])
            return carry

        lax.fori_loop(0, count, theirs, 0)
        base = base + count
    return base


def cross_kernel(state_ref, up_ref, down_ref, vel_in_ref, target_ref, source_ref, live_ref, lists_ref, vel_ref, ra, rb, ta, tb, oa):
    leaves = state_ref.shape[1]
    sides = (up_ref, down_ref)
    vel_ref[...] = vel_in_ref[...]

    def fetch(n, leaf, side, block, row):
        for c in range(2):
            ra[c, pl.ds(n, 1), :] = state_ref[c, pl.ds(leaf, 1), :]
        for c in range(3):
            rb[c, pl.ds(n, 1), :] = sides[side][block, c, pl.ds(row, 1), :]

    total = walk(target_ref, source_ref, live_ref, lists_ref, leaves, 0, fetch)

    def pair_group(i, carry):
        rows = pl.ds(pl.multiple_of(i * LANES, LANES), LANES)
        for c in range(2):
            ta[c] = ra[c, rows, :].T
        for c in range(3):
            tb[c] = rb[c, rows, :].T
        one_sided_lanes([ta.at[c] for c in range(2)], [tb.at[c] for c in range(3)], [oa.at[c] for c in range(2)])
        ra[0, rows, :] = oa[0].T * -biot_factor
        ra[1, rows, :] = oa[1].T * biot_factor
        return carry

    lax.fori_loop(0, (total + LANES - 1) // LANES, pair_group, 0)

    def spread(n, leaf, side, block, row):
        for c in range(2):
            vel_ref[c, pl.ds(leaf, 1), :] += ra[c, pl.ds(n, 1), :]

    walk(target_ref, source_ref, live_ref, lists_ref, leaves, 0, spread)


def pair_gap_kernel(x, y, lat, fwd):
    x = jnp.concatenate([x] * 4, axis=1) + lat[0:1, :]
    y = jnp.concatenate([y] * 4, axis=1) + lat[1:2, :]
    w = biot_factor * recip(x * x + y * y + 1.0)
    return dot3(-y * w, fwd[0], fwd[1]), dot3(x * w, fwd[0], fwd[1])


def wave_product(k, g, inv, sign):
    kr, ki, gr, gi = k[:, :256], k[:, 256:], g[:, :256], g[:, 256:]
    if sign < 0:
        wave = jnp.concatenate([kr * gr + ki * gi, kr * gi - ki * gr], axis=1)
    else:
        wave = jnp.concatenate([kr * gr - ki * gi, kr * gi + ki * gr], axis=1)
    return dot3(wave, inv[0], inv[1])


def cross_waves(gamma_ref, up_ref, down_ref, vel_in_ref, target_ref, source_ref, live_ref, lists_ref, own_anc, up_anc, down_anc, fwd, gam, inv, lat, vel_ref, rb, rd, ra):
    leaves = gamma_ref.shape[0]
    sides = (up_ref, down_ref)
    anchors = (up_anc, down_anc)
    vel_ref[...] = vel_in_ref[...]

    def fetch(n, leaf, side, block, row):
        rb[pl.ds(n, 1), :] = sides[side][block, pl.ds(row, 1), :]
        for c in range(2):
            gap = own_anc[2 * (leaf % 2) + c, leaf // 2] - anchors[side][block, 2 * (row % 2) + c, row // 2]
            rd[c, pl.ds(n, 1), :] = jnp.full((1, LANES), gap, f32)

    total = walk(target_ref, source_ref, live_ref, lists_ref, leaves, 1, fetch)

    def pair_group(i, carry):
        rows = pl.ds(pl.multiple_of(i * LANES, LANES), LANES)
        waves = dot3(rb[rows, :], gam[0], gam[1])
        for c, k in enumerate(pair_gap_kernel(rd[0, rows, :], rd[1, rows, :], lat, fwd)):
            ra[c, rows, :] = wave_product(k, waves, inv, 1)
        return carry

    lax.fori_loop(0, (total + LANES - 1) // LANES, pair_group, 0)

    def spread(n, leaf, side, block, row):
        for c in range(2):
            vel_ref[c, pl.ds(leaf, 1), :] += ra[c, pl.ds(n, 1), :]

    walk(target_ref, source_ref, live_ref, lists_ref, leaves, 1, spread)


def regroup_kernel(step, *refs):
    last = step == STEPS - 1
    refs = list(refs)
    take = lambda n: [refs.pop(0) for _ in range(n)]
    vel_ref, shift_ref, g_ref, anchor_ref, dest_ref = take(5)
    if not last:
        first_ref, second_ref, first_row_ref, second_row_ref, fwd, gam, inv, lat, own = take(9)
    (box_ref,) = take(1)
    if not last:
        gamma_ref, spread_ref, next_vel, up_ref, down_ref = take(5)
    px, py, pg, wx, out, nodes, outbox, send_sem, recv_sem, own_sem = take(10)
    if not last:
        block, own_ref, ra, rb, rd, ring_send, ring_recv = take(7)
        leaves = gamma_ref.shape[0]
        halves = lambda ref, m: [ref.at[m, pl.ds(0, leaves // 2)], ref.at[m, pl.ds(leaves // 2, leaves // 2 + 8)]]
        ring = Ring(block, own_ref, up_ref, down_ref, halves, ring_send, ring_recv)
    leaves = g_ref.shape[0]
    strip = lax.axis_index("strip")
    strips = outbox.shape[0]
    barrier = pltpu.get_barrier_semaphore()

    def greet(d, carry):
        pl.semaphore_signal(barrier, inc=1, device_id={"strip": lax.rem(strip + d, strips)})
        return carry

    lax.fori_loop(1, strips, greet, 0)
    if not last:
        for device in ({"grp": ring.left}, {"grp": ring.right}):
            pl.semaphore_signal(barrier, inc=1, device_id=device)

    def remesh(i, carry):
        rows = pl.ds(pl.multiple_of(i * LANES, LANES), LANES)
        for c, dst in ((0, px), (1, py)):
            dst[...] = (shift_ref[c, rows, :] + time_step * vel_ref[c, rows, :]).T
        pg[...] = g_ref[rows, :].T
        remesh_lanes(px, py, pg, wx, out)
        nodes[rows, :] = out[...].T
        return carry

    lax.fori_loop(0, leaves // LANES, remesh, 0)
    dest = dest_ref[...]
    named = jnp.where(lax.broadcasted_iota(jnp.int32, (strips, leaves), 0) == dest, 1.0, 0.0)
    rank = jnp.sum(named * dot(named.astype(bf16), earlier(leaves)), axis=0, keepdims=True)
    hot = [onehot(jnp.where(rank == float(r), named, 0.0) > 0.5) for r in range(2)]
    for r in range(2):
        outbox[:, r, :] = dot_exact(hot[r], nodes[...])
    lane = lax.broadcasted_iota(jnp.int32, (strips, LANES), 1)
    anchors = [dot_exact(hot[r], anchor_ref[...]) for r in range(2)]
    outbox[:, 2, :] = jnp.where(lane < LANES // 2, anchors[0], anchors[1])
    pl.semaphore_wait(barrier, strips - 1 + (0 if last else 2))

    def send(d, carry):
        to = lax.rem(strip + d, strips)
        pltpu.make_async_remote_copy(
            src_ref=outbox.at[to],
            dst_ref=box_ref.at[strip],
            send_sem=send_sem,
            recv_sem=recv_sem,
            device_id={"strip": to},
        ).start()
        return carry

    lax.fori_loop(1, strips, send, 0)
    mine = pltpu.make_async_copy(outbox.at[strip], box_ref.at[strip], own_sem)
    mine.start()
    mine.wait()
    rest = pl.ds(0, strips - 1)
    pltpu.make_async_copy(box_ref.at[rest], box_ref.at[rest], recv_sem).wait()
    pltpu.make_async_copy(outbox.at[rest], outbox.at[rest], send_sem).wait()
    if last:
        return
    for r in range(2):
        block[pl.ds(r, strips, stride=2), :] = box_ref[:, r, :]
    anchors = box_ref[:, 2, :]
    turned = anchors.T
    for q in range(4):
        block[leaves + q : leaves + q + 1, :] = turned[q * (LANES // 4) : q * (LANES // 4) + 1, :]
    block[leaves + 4 : leaves + 8, :] = jnp.zeros((4, LANES), f32)
    ring.first()
    rolled = pltpu.roll(anchors, LANES // 2, 1)
    spread_ref[pl.ds(0, strips, stride=2), :] = jnp.where(lane < LANES // 2, anchors, rolled)
    spread_ref[pl.ds(1, strips, stride=2), :] = jnp.where(lane < LANES // 2, rolled, anchors)
    gamma_ref[...] = block[pl.ds(0, leaves), :]
    field = dot3(gamma_ref[...], own[0], own[1])

    def pair_group(i):
        base = i * LANES

        def fetch(k):
            first = pl.ds(first_ref[base + k], 1)
            second = pl.ds(second_ref[base + k], 1)
            row = pl.ds(base + k, 1)
            ra[0, row, :] = gamma_ref[first, :]
            rb[0, row, :] = gamma_ref[second, :]
            rd[row, :] = spread_ref[first, :] - spread_ref[second, :]

        loop8(LANES, fetch)
        rows = pl.ds(base, LANES)
        gap = rd[rows, :]
        x = jnp.broadcast_to(gap[:, 0:1], (LANES, LANES))
        y = jnp.broadcast_to(gap[:, LANES // 4 : LANES // 4 + 1], (LANES, LANES))
        wa = dot3(ra[0, rows, :], gam[0], gam[1])
        wb = dot3(rb[0, rows, :], gam[0], gam[1])
        for c, k in enumerate(pair_gap_kernel(x, y, lat, fwd)):
            ra[c, rows, :] = wave_product(k, wb, inv, 1)
            rb[c, rows, :] = wave_product(k, wa, inv, -1)

    pair_group(0)
    ring.second()
    for i in range(1, leaves // LANES):
        pair_group(i)
    for c in range(2):
        next_vel[c] = (
            field[:, c * LANES : (c + 1) * LANES]
            + spread_rows(first_row_ref[...], ra[c])
            - spread_rows(second_row_ref[...], rb[c])
        )
    ring.third()
    ring.finish()


def shape(*sizes, dtype=f32):
    return jax.ShapeDtypeStruct(sizes, dtype)


def anywhere():
    return pl.BlockSpec(memory_space=pl.ANY)


def call(kernel, out_shape, in_specs, out_specs, scratch, **kw):
    return pl.pallas_call(
        kernel,
        out_shape=out_shape,
        in_specs=in_specs,
        out_specs=out_specs,
        scratch_shapes=scratch,
        compiler_params=pltpu.CompilerParams(vmem_limit_bytes=48 * 2**20, **kw),
    )


def run_local(state, first, second, target, source, live):
    leaves = state.shape[1]
    groups = lax.axis_size("grp")
    wide = (groups,) + state.shape
    dma = pltpu.SemaphoreType.DMA
    rows = lambda: pltpu.VMEM((3, leaves, LANES), f32)
    return call(
        local_kernel,
        (shape(2, leaves, LANES), shape(groups, 8, leaves, dtype=jnp.int32), shape(*wide), shape(*wide), shape(*wide)),
        [anywhere(), vspec(), sspec(), sspec(), vspec(), vspec(), vspec(), vspec(), sspec()],
        (vspec(), vspec(), anywhere(), anywhere(), anywhere()),
        [pltpu.VMEM((groups, 8, leaves), jnp.int32), tiles(3), tiles(3), tiles(2), tiles(2), rows(), rows()]
        + [dma((12,)), dma((12,)), dma((groups,)), dma((groups,))],
        collective_id=0,
        has_side_effects=True,
    )(state, state, first, second, first[None], second[None], target, source, live)[:4]


def run_cross(state, up, down, vel, target, source, live, lists):
    leaves = state.shape[1]
    most = (1 + up.shape[0]) * leaves
    return call(
        cross_kernel,
        shape(*vel.shape),
        [vspec()] * 4 + [sspec()] * 4,
        vspec(),
        [pltpu.VMEM((2, most, LANES), f32), pltpu.VMEM((3, most, LANES), f32), tiles(2), tiles(3), tiles(2)],
    )(state, up, down, vel, target, source, live, lists)


def run_cross_waves(gamma, up, down, vel, target, source, live, lists, anchors, tables):
    leaves = gamma.shape[0]
    most = (1 + up.shape[0]) * leaves
    fwd, gam, inv, lat, own = tables
    return call(
        cross_waves,
        shape(*vel.shape),
        [vspec()] * 4 + [sspec()] * 7 + [vspec()] * 4,
        vspec(),
        [pltpu.VMEM((most, LANES), f32), pltpu.VMEM((2, most, LANES), f32), pltpu.VMEM((2, most, LANES), f32)],
    )(gamma, up, down, vel, target, source, live, lists, *anchors, fwd, gam, inv, lat)


def run_regroup(step, vel, shifted, gamma, anchor, dest, *more):
    last = step == STEPS - 1
    leaves = gamma.shape[0]
    groups, strips = lax.axis_size("grp"), lax.axis_size("strip")
    dma = pltpu.SemaphoreType.DMA
    box = (strips, 3, LANES)
    out_shape = [shape(*box)]
    in_specs = [vspec()] * 5
    scratch = [tile(), tile(), tile(), pltpu.VMEM((2, WX, LANES), f32), tile(), pltpu.VMEM((leaves, LANES), f32)]
    scratch += [pltpu.VMEM(box, f32), dma, dma, dma]
    if not last:
        block = (leaves + 8, LANES)
        wide = (groups,) + block
        out_shape += [shape(leaves, LANES), shape(leaves, LANES), shape(2, leaves, LANES), shape(*wide), shape(*wide)]
        in_specs += [sspec(), sspec()] + [vspec()] * 7
        rows = lambda n: pltpu.VMEM((n, leaves, LANES), f32)
        scratch += [pltpu.VMEM(block, f32), pltpu.VMEM(wide, f32), rows(2), rows(2), pltpu.VMEM((leaves, LANES), f32)]
        scratch += [dma((12,)), dma((12,))]
    return call(
        functools.partial(regroup_kernel, step),
        tuple(out_shape),
        in_specs,
        (vspec(),) * len(out_shape),
        scratch,
        collective_id=1 + step,
        has_side_effects=True,
    )(vel, shifted, gamma, anchor, dest, *more)


def on_device(
    offsets,
    circulation,
    window_anchor,
    local_first,
    local_offset,
    cross_target,
    cross_source,
    cross_count,
    destination,
):
    leaves = circulation.shape[0]
    strips = lax.axis_size("strip")
    second = (local_first + local_offset) % leaves
    shifted = offsets.transpose(1, 0, 2)
    state = jnp.concatenate([shifted + window_anchor.T[:, :, None], circulation[None]], axis=0)
    anchor = jnp.tile(jnp.repeat(window_anchor, LANES // 4, axis=1), (1, 2))
    tables = [jnp.asarray(t) for t in fourier_tables()]
    lists = (cross_target, cross_source, cross_count)
    vel, inbox, up, down = run_local(state, local_first[0], second[0], *lists)
    vel = run_cross(state, up, down, vel, *lists, inbox)
    dest = destination[:, None, :, 0]
    _, gamma, anchor, vel, up, down = run_regroup(
        0, vel, shifted, circulation, anchor, dest[0],
        local_first[1], second[1], local_first[1:2], second[1:2], *tables,
    )
    own_anchors = anchor[:, :: LANES // 4].reshape(strips, 2, 4)[:, :, :2].reshape(strips, 4).T
    anchors = (own_anchors, up[:, leaves : leaves + 4], down[:, leaves : leaves + 4])
    vel = run_cross_waves(gamma, up, down, vel, *lists, inbox, anchors, tables)
    node = jnp.arange(LANES, dtype=jnp.int32)
    grid = jnp.stack([node // WY, node % WY]).astype(f32)
    shifted = jnp.broadcast_to(grid[:, None, :], vel.shape)
    (box,) = run_regroup(1, vel, shifted, gamma, anchor, dest[1])
    return box[:, :2].reshape(leaves, LANES), box[:, 2, :: LANES // 4].reshape(leaves, 2)


def solution(mesh):
    rows = P(("strip", "grp"))
    lists = P(None, ("strip", "grp"))
    return jax.shard_map(
        on_device,
        mesh=mesh,
        in_specs=(rows, rows, rows, lists, lists, lists, lists, lists, lists),
        out_specs=(rows, rows),
        check_vma=False,
    )
```

```python
import functools
import jax
import jax.numpy as jnp
import numpy as np
from jax import lax
from jax.experimental import pallas as pl
from jax.experimental.pallas import tpu as pltpu
from jax.sharding import PartitionSpec as P

WX = 8
WY = 16
STEPS = 2
time_step = 0.5
biot_factor = 0.15915494309189535
LANES = 128
f32 = jnp.float32
bf16 = jnp.bfloat16


def recip(x):
    return pl.reciprocal(x, approx=True)


def mutual_lanes(a_refs, b_refs, on_a, on_b, between):
    xa_ref, ya_ref, ga_ref = a_refs
    xb_ref, yb_ref, gb_ref = b_refs
    ua_ref, va_ref = on_a
    ub_ref, vb_ref = on_b
    ub_ref[...] = jnp.zeros_like(ub_ref)
    vb_ref[...] = jnp.zeros_like(vb_ref)
    zero = jnp.zeros((8, LANES), f32)

    def over_a(ia, carry):
        a0 = pl.multiple_of(ia * 8, 8)

        def over_b(ib, acc):
            acc = list(acc)
            rows = pl.ds(pl.multiple_of(ib * 8, 8), 8)
            xb, yb, gb = xb_ref[rows, :], yb_ref[rows, :], gb_ref[rows, :]
            ub, vb = ub_ref[rows, :], vb_ref[rows, :]
            for r in range(8):
                row = pl.ds(a0 + r, 1)
                dx = xa_ref[row, :] - xb
                dy = ya_ref[row, :] - yb
                w = recip(dx * dx + dy * dy + 1.0)
                tx = dx * w
                ty = dy * w
                acc[r] = acc[r] + gb * ty
                acc[8 + r] = acc[8 + r] + gb * tx
                ga = ga_ref[row, :]
                ub = ub + ga * ty
                vb = vb + ga * tx
            ub_ref[rows, :] = ub
            vb_ref[rows, :] = vb
            return tuple(acc)

        acc = lax.fori_loop(0, 16, over_b, (zero,) * 16, unroll=8)
        for r in range(8):
            ua_ref[pl.ds(a0 + r, 1), :] = jnp.sum(acc[r], axis=0, keepdims=True)
            va_ref[pl.ds(a0 + r, 1), :] = jnp.sum(acc[8 + r], axis=0, keepdims=True)
        return carry

    lax.fori_loop(0, 8, over_a, 0)
    between()
    lax.fori_loop(8, 16, over_a, 0)


def loop8(count, body):
    def eight(k, carry):
        for u in range(8):
            body(k * 8 + u)
        return carry

    lax.fori_loop(0, (count + 7) // 8, eight, 0)


def node_weight(distance):
    r = jnp.abs(distance)
    inner = 1.0 + r * r * (1.5 * r - 2.5)
    s = jnp.maximum(2.0 - r, 0.0)
    outer = (0.5 * s) * s * (1.0 - r)
    return jnp.where(r < 1.0, inner, outer)


def remesh_lanes(px_ref, py_ref, g_ref, wx_ref, nodes_ref):
    ix = lax.broadcasted_iota(jnp.int32, (WX, LANES), 0).astype(f32)
    iy = lax.broadcasted_iota(jnp.int32, (WX, LANES), 0).astype(f32)

    def over_p(p4, acc):
        acc = list(acc)
        for u in range(4):
            p = p4 * 4 + u
            row = pl.ds(p, 1)
            wx_ref[u] = node_weight(px_ref[row, :] - ix) * g_ref[row, :]
            y = py_ref[row, :] - iy
            wy = (node_weight(y), node_weight(y - 8.0))
            for i in range(WX):
                wxi = wx_ref[u, i : i + 1, :]
                for h in range(2):
                    acc[2 * i + h] = acc[2 * i + h] + wxi * wy[h]
        return tuple(acc)

    acc = lax.fori_loop(0, LANES // 4, over_p, (jnp.zeros((8, LANES), f32),) * 16)
    for i in range(16):
        nodes_ref[8 * i : 8 * i + 8, :] = acc[i]


def split(x):
    hi = x.astype(bf16)
    return hi, (x - hi.astype(f32)).astype(bf16)


def dot3(x, m_hi, m_lo):
    hi, lo = split(x)
    n = x.shape[0]
    both = dot(jnp.concatenate([hi, lo], axis=0), m_hi)
    return both[:n] + (both[n:] + dot(hi, m_lo))


def dot(a, b):
    return jnp.dot(a, b, preferred_element_type=f32)


@functools.cache
def fourier_tables():
    n1, n2 = 2 * WX - 1, 2 * WY - 1
    size = n1 * n2
    u = np.arange(n1)
    v = np.arange(n2)
    di = np.where(u < WX, u, u - n1)
    dj = np.where(v < WY, v, v - n2)
    DI, DJ = [t.reshape(-1).astype(np.float64) for t in np.meshgrid(di, dj, indexing="ij")]
    k1, k2 = [t.reshape(-1) for t in np.meshgrid(u, v, indexing="ij")]
    keep = [0]
    for m in range(1, size):
        mirror = ((-k1[m]) % n1) * n2 + ((-k2[m]) % n2)
        if m < mirror:
            keep.append(m)
    f1, f2 = k1[keep].astype(np.float64), k2[keep].astype(np.float64)
    nf = len(keep)

    def phase(i, j):
        return 2 * np.pi * (np.outer(i, f1) / n1 + np.outer(j, f2) / n2)

    forward = np.zeros((512, 512))
    p = phase(DI, DJ)
    forward[:size, :nf] = np.cos(p)
    forward[:size, 256 : 256 + nf] = -np.sin(p)
    node = np.arange(WX * WY)
    q = phase(node // WY, node % WY)
    gamma = np.zeros((128, 512))
    gamma[:, :nf] = np.cos(q)
    gamma[:, 256 : 256 + nf] = -np.sin(q)
    weight = np.full(nf, 2.0 / size)
    weight[0] = 1.0 / size
    inverse = np.zeros((512, 128))
    inverse[:nf] = weight[:, None] * np.cos(q).T
    inverse[256 : 256 + nf] = -weight[:, None] * np.sin(q).T
    lattice = np.zeros((8, 512))
    lattice[0, :size] = DI
    lattice[1, :size] = DJ
    ddx = (node // WY)[:, None] - (node // WY)[None, :]
    ddy = (node % WY)[:, None] - (node % WY)[None, :]
    w = biot_factor / (ddx * ddx + ddy * ddy + 1.0)
    own = np.concatenate([(-ddy * w).T, (ddx * w).T], axis=1)

    def halves(x):
        hi = x.astype(np.float32).astype(bf16)
        lo = (x - hi.astype(np.float64)).astype(np.float32).astype(bf16)
        return np.stack([hi, lo])

    return halves(forward), halves(gamma), halves(inverse), lattice.astype(np.float32), halves(own)


def vspec():
    return pl.BlockSpec(memory_space=pltpu.VMEM)


def sspec():
    return pl.BlockSpec(memory_space=pltpu.SMEM)


def tile():
    return pltpu.VMEM((LANES, LANES), f32)


def tiles(n):
    return pltpu.VMEM((n, LANES, LANES), f32)


def one_sided_lanes(a_refs, b_refs, on_a, chunks=2):
    xa_ref, ya_ref = a_refs
    xb_ref, yb_ref, gb_ref = b_refs
    ua_ref, va_ref = on_a
    zero = jnp.zeros((8, LANES), f32)

    def over_a(ia, carry):
        a0 = pl.multiple_of(ia * 8, 8)

        def over_b(chunk, u, acc):
            acc = list(acc)
            rows = pl.ds(pl.multiple_of(chunk * 64 + u * 8, 8), 8)
            xb, yb, gb = xb_ref[rows, :], yb_ref[rows, :], gb_ref[rows, :]
            for r in range(8):
                row = pl.ds(a0 + r, 1)
                dx = xa_ref[row, :] - xb
                dy = ya_ref[row, :] - yb
                w = gb * recip(dx * dx + (dy * dy + 1.0))
                acc[r] = acc[r] + dy * w
                acc[8 + r] = acc[8 + r] + dx * w
            return tuple(acc)

        def over_chunk(chunk, acc):
            for u in range(8):
                acc = over_b(chunk, u, acc)
            return acc

        acc = lax.fori_loop(0, chunks, over_chunk, (zero,) * 16)
        for r in range(8):
            ua_ref[pl.ds(a0 + r, 1), :] = jnp.sum(acc[r], axis=0, keepdims=True)
            va_ref[pl.ds(a0 + r, 1), :] = jnp.sum(acc[8 + r], axis=0, keepdims=True)
        return carry

    lax.fori_loop(0, 16, over_a, 0)


def onehot(condition):
    return jnp.where(condition, 1.0, 0.0).astype(bf16)


def dot_exact(hot, x):
    hi, rest = split(x)[0], None
    rest = x - hi.astype(f32)
    mid, lo = split(rest)
    return (dot(hot, hi) + dot(hot, mid)) + dot(hot, lo)


def dot_near(hot, x):
    hi, lo = split(x)
    return dot(hot, hi) + dot(hot, lo)


def spread_rows(index_row, x):
    leaves = index_row.shape[1]
    places = lax.broadcasted_iota(jnp.int32, (leaves, leaves), 0)
    return dot_near(onehot(places == index_row), x)


def earlier(n):
    return onehot(lax.broadcasted_iota(jnp.int32, (n, n), 0) < lax.broadcasted_iota(jnp.int32, (n, n), 1))


def sort_lists(target_ref, source_ref, live_ref, outbox):
    groups = outbox.shape[0]
    n = target_ref.shape[1]
    before = earlier(n)
    rows8 = lax.broadcasted_iota(jnp.int32, (8, n), 0)
    places = lax.broadcasted_iota(jnp.int32, (n, n), 0)
    k = lax.broadcasted_iota(jnp.int32, (1, n), 1)
    outbox[...] = jnp.zeros_like(outbox)
    for step in range(STEPS):
        source = source_ref[step : step + 1, :]
        owner = lax.shift_right_logical(source, n.bit_length() - 1)
        key = jnp.where(k < live_ref[0, step], owner, groups)
        row = jnp.bitwise_and(source, n - 1)
        mine = jnp.where(rows8 == key, 1.0, 0.0)
        place = jnp.sum(mine * dot(mine.astype(bf16), before), axis=0, keepdims=True).astype(jnp.int32)
        values = jnp.where(rows8 == 0, target_ref[step : step + 1, :], jnp.where(rows8 == 1, row, 0))
        values = values.astype(f32).astype(bf16)
        count = jnp.sum(mine, axis=1, keepdims=True).astype(jnp.int32)
        for b in range(groups):
            hot = onehot((places == place) & (key == b))
            found = lax.dot_general(values, hot, (((1,), (1,)), ((), ())), preferred_element_type=f32)
            outbox[b, 2 * step : 2 * step + 2, :] = found[0:2, :].astype(jnp.int32)
            outbox[b, 4 + step : 5 + step, :] = jnp.broadcast_to(count[b : b + 1, :], (1, n))


class Ring:
    def __init__(self, block, own, up, down, part, chunk, send_sem, recv_sem):
        start, size, first = chunk
        self.block = part(block, start, size)
        view = lambda ref: lambda member: part(ref, start, size, member)
        self.own, self.up, self.down = view(own), view(up), view(down)
        self.halves = (
            lambda member: part(own, start, first, member),
            lambda member: part(own, start + first, size - first, member),
        )
        self.send_sem, self.recv_sem = send_sem, recv_sem
        self.grp = lax.axis_index("grp")
        groups = lax.axis_size("grp")
        self.right = lax.rem(self.grp + 1, groups)
        self.left = lax.rem(self.grp + groups - 1, groups)
        self.across = lax.rem(self.grp + 2, groups)
        strip, strips = lax.axis_index("strip"), lax.axis_size("strip")
        self.above = lax.rem(strip + 1, strips)
        self.below = lax.rem(strip + strips - 1, strips)
        self.sent = []

    def send(self, src, dst, device, slot):
        copy = pltpu.make_async_remote_copy(
            src_ref=src,
            dst_ref=dst,
            send_sem=self.send_sem.at[slot],
            recv_sem=self.recv_sem.at[slot],
            device_id=device,
        )
        copy.start()
        self.sent.append(copy)
        return copy

    def to_strips(self, src, member, slot):
        return [
            self.send(src, self.down(member), {"strip": self.above}, slot),
            self.send(src, self.up(member), {"strip": self.below}, slot + 1),
        ]

    def first(self):
        self.from_left = self.send(self.block, self.own(self.grp), {"grp": self.right}, 0)
        self.from_right = self.send(self.block, self.own(self.grp), {"grp": self.left}, 1)
        self.last = self.to_strips(self.block, self.grp, 2)

    def second(self):
        self.from_left.wait_recv()
        half = self.halves[0](self.left)
        self.half_a = self.send(half, half, {"grp": self.right}, 4)
        self.last += self.to_strips(self.own(self.left), self.left, 5)
        self.from_right.wait_recv()
        half = self.halves[1](self.right)
        self.half_b = self.send(half, half, {"grp": self.left}, 7)
        self.last += self.to_strips(self.own(self.right), self.right, 8)

    def third(self):
        self.half_a.wait_recv()
        self.half_b.wait_recv()
        self.last += self.to_strips(self.own(self.across), self.across, 10)

    def finish(self):
        for copy in self.last:
            copy.wait_recv()
        for copy in self.sent:
            copy.wait_send()


class Rings:
    def __init__(self, block, own, up, down, part, chunks, send_sem, recv_sem):
        self.rings = [
            Ring(block, own, up, down, part, chunk, send_sem.at[i], recv_sem.at[i]) for i, chunk in enumerate(chunks)
        ]

    def first(self):
        for ring in self.rings:
            ring.first()

    def second(self):
        for ring in self.rings:
            ring.second()

    def third(self):
        for ring in self.rings:
            ring.third()

    def finish(self):
        for ring in self.rings:
            ring.finish()


def local_kernel(
    offset_in,
    gamma_in,
    anchor_in,
    first_in,
    shift_in,
    target_in,
    source_in,
    live_ref,
    state_ref,
    vel_ref,
    lists_ref,
    first_out,
    second_out,
    target_ref,
    source_ref,
    up_ref,
    down_ref,
    own_ref,
    offset_ref,
    gamma_ref,
    anchor_ref,
    shift_ref,
    first_ref,
    second_ref,
    outbox,
    ta,
    tb,
    oa,
    ob,
    ra,
    rb,
    load_sem,
    send_sem,
    recv_sem,
    list_send,
    list_recv,
):
    loaded = load_tables(
        [
            (offset_in, offset_ref),
            (gamma_in, gamma_ref),
            (anchor_in, anchor_ref),
            (first_in, first_out),
            (shift_in, shift_ref),
            (target_in, target_ref),
            (source_in, source_ref),
            (first_in, first_ref),
            (shift_in, second_ref),
        ],
        load_sem,
    )
    leaves = gamma_ref.shape[0]
    blocks = range(leaves // LANES)
    part = lambda ref, start, size, *member: ref.at[(*member, slice(None), pl.ds(start, size))]
    cut = leaves // 2
    chunks = [(0, cut, cut // 2), (cut, cut, cut // 2)]
    rings = Rings(state_ref, own_ref, up_ref, down_ref, part, chunks, send_sem, recv_sem)
    ring = rings.rings[0]
    groups = lists_ref.shape[0]
    barrier = pltpu.get_barrier_semaphore()
    for device in ({"grp": ring.left}, {"grp": ring.right}, {"strip": ring.above}):
        pl.semaphore_signal(barrier, inc=1, device_id=device)
    for j in range(groups):
        pl.semaphore_signal(barrier, inc=1, device_id={"strip": ring.below, "grp": j})
    loaded()
    second_out[...] = jnp.bitwise_and(first_out[...] + shift_ref[...], leaves - 1)
    for h in blocks:
        rows = pl.ds(h * LANES, LANES)
        for c in range(2):
            column = jnp.broadcast_to(anchor_ref[c : c + 1, h * LANES : (h + 1) * LANES], (LANES, LANES)).T
            state_ref[c, rows, :] = offset_ref[rows, c, :] + column
        state_ref[2, rows, :] = gamma_ref[rows, :]
    pl.semaphore_wait(barrier, 3 + groups)
    rings.first()
    sort_lists(target_ref, source_ref, live_ref, outbox)
    mail = []
    for j in range(groups):
        peer = lax.rem(ring.grp + j, groups)
        copy = pltpu.make_async_remote_copy(
            src_ref=outbox.at[peer],
            dst_ref=lists_ref.at[ring.grp],
            send_sem=list_send.at[j],
            recv_sem=list_recv.at[j],
            device_id={"strip": ring.above, "grp": peer},
        )
        copy.start()
        mail.append(copy)

    def self_group(i, carry):
        rows = pl.ds(pl.multiple_of(i * LANES, LANES), LANES)
        for c in range(3):
            ta[c] = state_ref[c, rows, :].T
        one_sided_lanes((ta.at[0], ta.at[1]), (ta.at[0], ta.at[1], ta.at[2]), (oa.at[0], oa.at[1]))
        vel_ref[0, rows, :] = oa[0].T * -biot_factor
        vel_ref[1, rows, :] = oa[1].T * biot_factor
        return carry

    def pair_group(i, between):
        base = i * LANES
        rows = pl.ds(base, LANES)

        def fetch(k):
            first = first_ref[0, base + k]
            second = jnp.bitwise_and(first + second_ref[0, base + k], leaves - 1)
            for c in range(3):
                ra[c, pl.ds(base + k, 1), :] = state_ref[c, pl.ds(first, 1), :]
                rb[c, pl.ds(base + k, 1), :] = state_ref[c, pl.ds(second, 1), :]

        loop8(LANES, fetch)
        for c in range(3):
            ta[c] = ra[c, rows, :].T
            tb[c] = rb[c, rows, :].T
        mutual_lanes(
            [ta.at[c] for c in range(3)],
            [tb.at[c] for c in range(3)],
            [oa.at[c] for c in range(2)],
            [ob.at[c] for c in range(2)],
            between,
        )
        ra[0, rows, :] = oa[0].T * -biot_factor
        ra[1, rows, :] = oa[1].T * biot_factor
        rb[0, rows, :] = ob[0].T * biot_factor
        rb[1, rows, :] = ob[1].T * -biot_factor

    lax.fori_loop(0, leaves // LANES, self_group, 0)
    rings.second()
    for i in blocks:
        pair_group(i, rings.third if i == 0 else lambda: None)
    for c in range(2):
        vel_ref[c] += spread_rows(first_out[0:1, :], ra[c]) + spread_rows(second_out[0:1, :], rb[c])
    rings.finish()
    for copy in mail:
        copy.wait()


def walk(target_ref, source_ref, live_ref, lists_ref, leaves, step, visit):
    live = live_ref[0, step]
    shift = leaves.bit_length() - 1

    def mine(k):
        source = source_ref[step, k]
        block, row = lax.shift_right_logical(source, shift), jnp.bitwise_and(source, leaves - 1)
        visit(k, jnp.where(k < live, target_ref[step, k], leaves), 0, block, row)

    loop8(live, mine)
    base = live
    for g in range(lists_ref.shape[0]):
        count = lists_ref[g, 4 + step, 0]

        def theirs(k, g=g, base=base, count=count):
            leaf = jnp.where(k < count, lists_ref[g, 2 * step + 1, k], leaves)
            visit(base + k, leaf, 1, g, lists_ref[g, 2 * step, k])

        loop8(count, theirs)
        base = base + count
    return base


def cross_kernel(state_ref, up_ref, down_ref, vel_in_ref, target_ref, source_ref, live_ref, lists_ref, vel_ref, ra, rb, ta, tb, oa, total_ref):
    leaves = state_ref.shape[1]
    sides = (up_ref, down_ref)
    for c in range(2):
        total_ref[c, pl.ds(0, leaves), :] = vel_in_ref[c]

    def fetch(n, leaf, side, block, row):
        own = jnp.minimum(leaf, leaves - 1)
        for c in range(2):
            ra[c, pl.ds(n, 1), :] = state_ref[c, pl.ds(own, 1), :]
        for c in range(3):
            rb[c, pl.ds(n, 1), :] = sides[side][block, c, pl.ds(row, 1), :]

    total = walk(target_ref, source_ref, live_ref, lists_ref, leaves, 0, fetch)

    def pair_group(i, carry):
        rows = pl.ds(pl.multiple_of(i * LANES, LANES), LANES)
        half = LANES // 2
        few = total - i * LANES <= half

        @pl.when(few)
        def _():
            low = pl.ds(pl.multiple_of(i * LANES, LANES), half)
            high = pl.ds(pl.multiple_of(i * LANES + half, half), half)
            for c in range(2):
                ra[c, high, :] = ra[c, low, :]
            for c in range(3):
                rb[c, high, :] = pltpu.roll(rb[c, low, :], half, 1)

        for c in range(2):
            ta[c] = ra[c, rows, :].T
        for c in range(3):
            tb[c] = rb[c, rows, :].T
        one_sided_lanes(
            [ta.at[c] for c in range(2)],
            [tb.at[c] for c in range(3)],
            [oa.at[c] for c in range(2)],
            jnp.where(few, 1, 2),
        )
        for c, sign in ((0, -biot_factor), (1, biot_factor)):
            found = oa[c].T * sign
            ra[c, rows, :] = found
            ra[c, pl.ds(pl.multiple_of(i * LANES, LANES), half), :] = found[:half] + jnp.where(few, found[half:], 0.0)
        return carry

    lax.fori_loop(0, (total + LANES - 1) // LANES, pair_group, 0)

    def spread(n, leaf, side, block, row):
        for c in range(2):
            total_ref[c, pl.ds(leaf, 1), :] += ra[c, pl.ds(n, 1), :]

    walk(target_ref, source_ref, live_ref, lists_ref, leaves, 0, spread)
    for c in range(2):
        vel_ref[c] = total_ref[c, pl.ds(0, leaves), :]


def lattice_waves(x, y, lat, fwd):
    n = x.shape[0]
    x = jnp.concatenate([x] * 4, axis=1) + lat[0:1, :]
    y = jnp.concatenate([y] * 4, axis=1) + lat[1:2, :]
    w = biot_factor * recip(x * x + y * y + 1.0)
    waves = dot3(jnp.concatenate([-y * w, x * w], axis=0), fwd[0], fwd[1])
    return waves[:n], waves[n:]


def wave_product(k, g, sign):
    kr, ki, gr, gi = k[:, :256], k[:, 256:], g[:, :256], g[:, 256:]
    if sign < 0:
        return jnp.concatenate([kr * gr + ki * gi, kr * gi - ki * gr], axis=1)
    return jnp.concatenate([kr * gr - ki * gi, kr * gi + ki * gr], axis=1)


def load_tables(pairs, sem):
    copies = [pltpu.make_async_copy(src, dst, sem.at[i]) for i, (src, dst) in enumerate(pairs)]
    for copy in copies:
        copy.start()

    def wait():
        for copy in copies:
            copy.wait()

    return wait


def spread_anchors(anchor_ref, half):
    cols = slice(half * LANES, (half + 1) * LANES)
    part = [jnp.broadcast_to(anchor_ref[c : c + 1, cols], (LANES // 4, LANES)) for c in range(2)]
    return jnp.concatenate(part + part, axis=0).T


def cross_waves(
    spread_ref,
    up_ref,
    down_ref,
    vel_in_ref,
    target_ref,
    source_ref,
    live_ref,
    lists_ref,
    fwd_in,
    gam_in,
    inv_in,
    lat,
    vel_ref,
    rb,
    rd,
    ra,
    total_ref,
    far_anc,
    fwd,
    gam,
    inv,
    sem,
):
    leaves = vel_in_ref.shape[1]
    sides = (up_ref, down_ref)
    ready = load_tables([(fwd_in, fwd), (gam_in, gam), (inv_in, inv)], sem)
    quarter = LANES // 4
    for side in range(2):
        for b in range(up_ref.shape[0]):
            lines = [
                jnp.broadcast_to(sides[side][b, leaves + q : leaves + q + 1, :], (quarter, LANES)) for q in range(4)
            ]
            anchors = jnp.concatenate(lines, axis=0).T
            far_anc[side, b, pl.ds(0, LANES, stride=2), :] = anchors
            far_anc[side, b, pl.ds(1, LANES, stride=2), :] = pltpu.roll(anchors, LANES // 2, 1)
    for c in range(2):
        total_ref[c, pl.ds(0, leaves), :] = vel_in_ref[c]

    def fetch(n, leaf, side, block, row):
        rb[pl.ds(n, 1), :] = sides[side][block, pl.ds(row, 1), :]
        own = jnp.minimum(leaf, leaves - 1)
        rd[pl.ds(n, 1), :] = spread_ref[pl.ds(own, 1), :] - far_anc[side, block, pl.ds(row, 1), :]

    total = walk(target_ref, source_ref, live_ref, lists_ref, leaves, 1, fetch)
    ready()

    def pair_group(i, carry):
        rows = pl.ds(pl.multiple_of(i * LANES, LANES), LANES)
        waves = dot3(rb[rows, :], gam[0], gam[1])
        gap = rd[rows, :]
        x = jnp.broadcast_to(gap[:, 0:1], (LANES, LANES))
        y = jnp.broadcast_to(gap[:, quarter : quarter + 1], (LANES, LANES))
        products = [wave_product(k, waves, 1) for k in lattice_waves(x, y, lat, fwd)]
        found = dot3(jnp.concatenate(products, axis=0), inv[0], inv[1])
        ra[0, rows, :] = found[:LANES]
        ra[1, rows, :] = found[LANES:]
        return carry

    lax.fori_loop(0, (total + LANES - 1) // LANES, pair_group, 0)

    def spread(n, leaf, side, block, row):
        for c in range(2):
            total_ref[c, pl.ds(leaf, 1), :] += ra[c, pl.ds(n, 1), :]

    walk(target_ref, source_ref, live_ref, lists_ref, leaves, 1, spread)
    for c in range(2):
        vel_ref[c] = total_ref[c, pl.ds(0, leaves), :]


def regroup_kernel(step, *refs):
    last = step == STEPS - 1
    refs = list(refs)
    take = lambda n: [refs.pop(0) for _ in range(n)]
    vel_ref, shift_ref, g_ref, anchor_ref, dest_ref = take(5)
    leaves = vel_ref.shape[1]
    if not last:
        first_ref, second_ref, first_row_ref, second_row_ref, fwd_in, gam_in, inv_in, lat, own_in = take(9)
        block, spread_ref, next_vel, up_ref, down_ref = take(5)
    else:
        gamma_ref, final_ref = take(2)
    px, py, pg, wx, out, nodes, outbox, box_ref, send_sem, recv_sem, own_sem = take(11)
    if not last:
        own_ref, ra, rb, rd, fwd, gam, inv, own, ring_send, ring_recv, table_sem = take(11)
        ready = load_tables([(fwd_in, fwd), (gam_in, gam), (inv_in, inv), (own_in, own)], table_sem)
    else:
        (spread_ref,) = take(1)
    if not last:
        part = lambda ref, start, size, *member: ref.at[(*member, pl.ds(start, size))]
        cut = leaves // 2
        chunks = [(0, cut, cut // 2), (cut, cut + 8, cut // 2)]
        rings = Rings(block, own_ref, up_ref, down_ref, part, chunks, ring_send, ring_recv)
        ring = rings.rings[0]
    strip = lax.axis_index("strip")
    strips = outbox.shape[0]
    barrier = pltpu.get_barrier_semaphore()

    def greet(d, carry):
        pl.semaphore_signal(barrier, inc=1, device_id={"strip": jnp.bitwise_and(strip + d, strips - 1)})
        return carry

    lax.fori_loop(1, strips, greet, 0, unroll=8)
    if not last:
        for device in ({"grp": ring.left}, {"grp": ring.right}):
            pl.semaphore_signal(barrier, inc=1, device_id=device)

    def remesh(i, carry):
        rows = pl.ds(pl.multiple_of(i * LANES, LANES), LANES)
        for c, dst in ((0, px), (1, py)):
            if last:
                node = lax.broadcasted_iota(jnp.int32, (LANES, LANES), 0)
                node = jnp.bitwise_and(node, WY - 1) if c else lax.shift_right_logical(node, WY.bit_length() - 1)
                dst[...] = node.astype(f32) + (time_step * vel_ref[c, rows, :]).T
            else:
                dst[...] = (shift_ref[rows, c, :] + time_step * vel_ref[c, rows, :]).T
        pg[...] = g_ref[rows, :].T
        remesh_lanes(px, py, pg, wx, out)
        nodes[rows, :] = out[...].T
        return carry

    lax.fori_loop(0, leaves // LANES, remesh, 0)
    dest = dest_ref[step]
    named = jnp.where(lax.broadcasted_iota(jnp.int32, (strips, leaves), 0) == dest, 1.0, 0.0)
    rank = jnp.sum(named * dot(named.astype(bf16), earlier(leaves)), axis=0, keepdims=True)
    hot = [onehot(jnp.where(rank == float(r), named, 0.0) > 0.5) for r in range(2)]
    for r in range(2):
        outbox[:, r, :] = dot_exact(hot[r], nodes[...])
    lane = lax.broadcasted_iota(jnp.int32, (strips, LANES), 1)
    if last:
        spread = anchor_ref[...]
    else:
        spread = jnp.concatenate([spread_anchors(anchor_ref, h) for h in range(leaves // LANES)], axis=0)
    anchors = [dot_exact(hot[r], spread) for r in range(2)]
    outbox[:, 2, :] = jnp.where(lane < LANES // 2, anchors[0], anchors[1])
    pl.semaphore_wait(barrier, strips - 1 + (0 if last else 2))

    def send(d, carry):
        to = jnp.bitwise_and(strip + d, strips - 1)
        pltpu.make_async_remote_copy(
            src_ref=outbox.at[to],
            dst_ref=box_ref.at[strip],
            send_sem=send_sem,
            recv_sem=recv_sem,
            device_id={"strip": to},
        ).start()
        return carry

    lax.fori_loop(1, strips, send, 0, unroll=8)
    mine = pltpu.make_async_copy(outbox.at[strip], box_ref.at[strip], own_sem)
    mine.start()
    mine.wait()
    rest = pl.ds(0, strips - 1)
    pltpu.make_async_copy(box_ref.at[rest], box_ref.at[rest], recv_sem).wait()
    pltpu.make_async_copy(outbox.at[rest], outbox.at[rest], send_sem).wait()
    anchors = box_ref[:, 2, :]
    rolled = pltpu.roll(anchors, LANES // 2, 1)
    if last:
        for r in range(2):
            gamma_ref[pl.ds(r, strips, stride=2), :] = box_ref[:, r, :]
        spread_ref[pl.ds(0, strips, stride=2), :] = anchors
        spread_ref[pl.ds(1, strips, stride=2), :] = rolled
        for h in range(leaves // LANES):
            turned = spread_ref[pl.ds(h * LANES, LANES), :].T
            for c in range(2):
                row = turned[c * (LANES // 4) : c * (LANES // 4) + 1, :]
                final_ref[c : c + 1, h * LANES : (h + 1) * LANES] = row
        return
    for r in range(2):
        block[pl.ds(r, strips, stride=2), :] = box_ref[:, r, :]
    turned = anchors.T
    for q in range(4):
        block[leaves + q : leaves + q + 1, :] = turned[q * (LANES // 4) : q * (LANES // 4) + 1, :]
    block[leaves + 4 : leaves + 8, :] = jnp.zeros((4, LANES), f32)
    rings.first()
    spread_ref[pl.ds(0, strips, stride=2), :] = jnp.where(lane < LANES // 2, anchors, rolled)
    spread_ref[pl.ds(1, strips, stride=2), :] = jnp.where(lane < LANES // 2, rolled, anchors)
    ready()
    field = dot3(block[pl.ds(0, leaves), :], own[0], own[1])

    def pair_group(i, between):
        base = i * LANES

        def fetch(k):
            first = pl.ds(first_ref[1, base + k], 1)
            second = pl.ds(second_ref[1, base + k], 1)
            row = pl.ds(base + k, 1)
            ra[0, row, :] = block[first, :]
            rb[0, row, :] = block[second, :]
            rd[row, :] = spread_ref[first, :] - spread_ref[second, :]

        loop8(LANES, fetch)
        between()
        rows = pl.ds(base, LANES)
        gap = rd[rows, :]
        x = jnp.broadcast_to(gap[:, 0:1], (LANES, LANES))
        y = jnp.broadcast_to(gap[:, LANES // 4 : LANES // 4 + 1], (LANES, LANES))
        waves = dot3(jnp.concatenate([ra[0, rows, :], rb[0, rows, :]], axis=0), gam[0], gam[1])
        wa, wb = waves[:LANES], waves[LANES:]
        kernels = lattice_waves(x, y, lat, fwd)
        products = [wave_product(k, wb, 1) for k in kernels] + [wave_product(k, wa, -1) for k in kernels]
        found = dot3(jnp.concatenate(products, axis=0), inv[0], inv[1])
        for c in range(2):
            ra[c, rows, :] = found[c * LANES : (c + 1) * LANES]
            rb[c, rows, :] = found[(2 + c) * LANES : (3 + c) * LANES]

    for i in range(leaves // LANES):
        pair_group(i, (rings.second, rings.third)[i] if i < 2 else lambda: None)
    for c in range(2):
        next_vel[c] = (
            field[:, c * LANES : (c + 1) * LANES]
            + spread_rows(first_row_ref[1:2, :], ra[c])
            - spread_rows(second_row_ref[1:2, :], rb[c])
        )
    rings.finish()


def shape(*sizes, dtype=f32):
    return jax.ShapeDtypeStruct(sizes, dtype)


def anywhere():
    return pl.BlockSpec(memory_space=pl.ANY)


def call(kernel, out_shape, in_specs, out_specs, scratch, **kw):
    return pl.pallas_call(
        kernel,
        out_shape=out_shape,
        in_specs=in_specs,
        out_specs=out_specs,
        scratch_shapes=scratch,
        compiler_params=pltpu.CompilerParams(vmem_limit_bytes=48 * 2**20, **kw),
    )


def run_local(offsets, gamma, anchor, first, shift, target, source, live):
    leaves = gamma.shape[0]
    groups = lax.axis_size("grp")
    state = (3, leaves, LANES)
    wide = (groups,) + state
    dma = pltpu.SemaphoreType.DMA
    rows = lambda: pltpu.VMEM(state, f32)
    pairs = first.shape
    ints = shape(*pairs, dtype=jnp.int32)
    return call(
        local_kernel,
        (shape(*state), shape(2, leaves, LANES), shape(groups, 8, leaves, dtype=jnp.int32))
        + (ints,) * 4
        + (shape(*wide),) * 3,
        [pl.BlockSpec(memory_space=pltpu.HBM)] * 7 + [sspec()],
        (vspec(),) * 7 + (anywhere(),) * 3,
        [pltpu.VMEM(offsets.shape, f32), pltpu.VMEM(gamma.shape, f32), pltpu.VMEM(anchor.shape, f32)]
        + [pltpu.VMEM(pairs, jnp.int32), pltpu.SMEM(pairs, jnp.int32), pltpu.SMEM(pairs, jnp.int32)]
        + [pltpu.VMEM((groups, 8, leaves), jnp.int32), tiles(3), tiles(3), tiles(2), tiles(2), rows(), rows()]
        + [dma((9,)), dma((2, 12)), dma((2, 12)), dma((groups,)), dma((groups,))],
        collective_id=0,
        has_side_effects=True,
    )(offsets, gamma, anchor, first, shift, target, source, live)[:9]


def run_cross(state, up, down, vel, target, source, live, lists):
    leaves = state.shape[1]
    most = (1 + up.shape[0]) * leaves + LANES
    return call(
        cross_kernel,
        shape(*vel.shape),
        [vspec()] * 4 + [sspec()] * 4,
        vspec(),
        [pltpu.VMEM((2, most, LANES), f32), pltpu.VMEM((3, most, LANES), f32), tiles(2), tiles(3), tiles(2)]
        + [pltpu.VMEM((2, leaves + 8, LANES), f32)],
    )(state, up, down, vel, target, source, live, lists)


def run_cross_waves(spread, up, down, vel, target, source, live, lists, tables):
    leaves = vel.shape[1]
    groups = up.shape[0]
    most = (1 + groups) * leaves + 8
    fwd, gam, inv, lat, own = tables
    return call(
        cross_waves,
        shape(*vel.shape),
        [vspec()] * 4 + [sspec()] * 4 + [anywhere()] * 3 + [vspec()],
        vspec(),
        [pltpu.VMEM((most, LANES), f32), pltpu.VMEM((most, LANES), f32), pltpu.VMEM((2, most, LANES), f32)]
        + [pltpu.VMEM((2, leaves + 8, LANES), f32), pltpu.VMEM((2, groups, leaves, LANES), f32)]
        + [pltpu.VMEM(t.shape, bf16) for t in (fwd, gam, inv)]
        + [pltpu.SemaphoreType.DMA((3,))],
    )(spread, up, down, vel, target, source, live, lists, fwd, gam, inv, lat)


def run_regroup(step, vel, shifted, gamma, anchor, dest, *more):
    last = step == STEPS - 1
    leaves = vel.shape[1]
    groups, strips = lax.axis_size("grp"), lax.axis_size("strip")
    dma = pltpu.SemaphoreType.DMA
    box = (strips, 3, LANES)
    in_specs = [vspec()] * 5
    scratch = [tile(), tile(), tile(), pltpu.VMEM((4, WX, LANES), f32), tile(), pltpu.VMEM((leaves, LANES), f32)]
    scratch += [pltpu.VMEM(box, f32), pltpu.VMEM(box, f32), dma, dma, dma]
    if last:
        out_shape = [shape(leaves, LANES), shape(2, leaves)]
        scratch += [pltpu.VMEM((leaves, LANES), f32)]
    else:
        block = (leaves + 8, LANES)
        wide = (groups,) + block
        out_shape = [shape(*block), shape(leaves, LANES), shape(2, leaves, LANES), shape(*wide), shape(*wide)]
        in_specs += [sspec(), sspec(), vspec(), vspec()] + [anywhere()] * 3 + [vspec(), anywhere()]
        rows = lambda n: pltpu.VMEM((n, leaves, LANES), f32)
        scratch += [pltpu.VMEM(wide, f32), rows(2), rows(2), pltpu.VMEM((leaves, LANES), f32)]
        scratch += [pltpu.VMEM(more[i].shape, bf16) for i in (4, 5, 6, 8)]
        scratch += [dma((2, 12)), dma((2, 12)), dma((4,))]
    return call(
        functools.partial(regroup_kernel, step),
        tuple(out_shape),
        in_specs,
        (vspec(),) * len(out_shape),
        scratch,
        collective_id=1 + step,
        has_side_effects=True,
    )(vel, shifted, gamma, anchor, dest, *more)


def on_device(
    offsets,
    circulation,
    window_anchor,
    local_first,
    local_offset,
    cross_target,
    cross_source,
    cross_count,
    destination,
):
    anchor = window_anchor.T
    dest = destination.transpose(0, 2, 1)
    tables = [jnp.asarray(t) for t in fourier_tables()]
    live = cross_count.T
    state, vel, inbox, first, second, target, source, up, down = run_local(
        offsets, circulation, anchor, local_first, local_offset, cross_target, cross_source, live
    )
    lists = (target, source, live, inbox)
    vel = run_cross(state, up, down, vel, *lists)
    block, spread, vel, up, down = run_regroup(
        0, vel, offsets, circulation, anchor, dest, first, second, first, second, *tables
    )
    vel = run_cross_waves(spread, up, down, vel, *lists, tables)
    gamma, anchor = run_regroup(1, vel, block, block, spread, dest)
    return gamma, anchor.T


def solution(mesh):
    rows = P(("strip", "grp"))
    lists = P(None, ("strip", "grp"))
    return jax.shard_map(
        on_device,
        mesh=mesh,
        in_specs=(rows, rows, rows, lists, lists, lists, lists, lists, lists),
        out_specs=(rows, rows),
        check_vma=False,
    )
```

```python
import functools
import jax
import jax.numpy as jnp
import numpy as np
from jax import lax
from jax.experimental import pallas as pl
from jax.experimental.pallas import tpu as pltpu
from jax.sharding import PartitionSpec as P

WX = 8
WY = 16
STEPS = 2
time_step = 0.5
biot_factor = 0.15915494309189535
LANES = 128
f32 = jnp.float32
bf16 = jnp.bfloat16


def recip(x):
    return pl.reciprocal(x, approx=True)


def mutual_lanes(a_refs, b_refs, on_a, on_b, between):
    xa_ref, ya_ref, ga_ref = a_refs
    xb_ref, yb_ref, gb_ref = b_refs
    ua_ref, va_ref = on_a
    ub_ref, vb_ref = on_b
    ub_ref[...] = jnp.zeros_like(ub_ref)
    vb_ref[...] = jnp.zeros_like(vb_ref)
    zero = jnp.zeros((8, LANES), f32)

    def over_a(ia, carry):
        a0 = pl.multiple_of(ia * 8, 8)

        def over_b(ib, acc):
            acc = list(acc)
            rows = pl.ds(pl.multiple_of(ib * 8, 8), 8)
            xb, yb, gb = xb_ref[rows, :], yb_ref[rows, :], gb_ref[rows, :]
            ub, vb = ub_ref[rows, :], vb_ref[rows, :]
            for r in range(8):
                row = pl.ds(a0 + r, 1)
                dx = xa_ref[row, :] - xb
                dy = ya_ref[row, :] - yb
                w = recip(dx * dx + dy * dy + 1.0)
                tx = dx * w
                ty = dy * w
                acc[r] = acc[r] + gb * ty
                acc[8 + r] = acc[8 + r] + gb * tx
                ga = ga_ref[row, :]
                ub = ub + ga * ty
                vb = vb + ga * tx
            ub_ref[rows, :] = ub
            vb_ref[rows, :] = vb
            return tuple(acc)

        acc = lax.fori_loop(0, 16, over_b, (zero,) * 16, unroll=8)
        for r in range(8):
            ua_ref[pl.ds(a0 + r, 1), :] = jnp.sum(acc[r], axis=0, keepdims=True)
            va_ref[pl.ds(a0 + r, 1), :] = jnp.sum(acc[8 + r], axis=0, keepdims=True)
        return carry

    lax.fori_loop(0, 8, over_a, 0)
    between()
    lax.fori_loop(8, 16, over_a, 0)


def loop8(count, body):
    def eight(k, carry):
        for u in range(8):
            body(k * 8 + u)
        return carry

    lax.fori_loop(0, (count + 7) // 8, eight, 0)


def node_weight(distance):
    r = jnp.abs(distance)
    inner = 1.0 + r * r * (1.5 * r - 2.5)
    s = jnp.maximum(2.0 - r, 0.0)
    outer = (0.5 * s) * s * (1.0 - r)
    return jnp.where(r < 1.0, inner, outer)


def remesh_lanes(px_ref, py_ref, g_ref, wx_ref, nodes_ref):
    ix = lax.broadcasted_iota(jnp.int32, (WX, LANES), 0).astype(f32)
    iy = lax.broadcasted_iota(jnp.int32, (WX, LANES), 0).astype(f32)

    def over_p(p4, acc):
        acc = list(acc)
        for u in range(4):
            p = p4 * 4 + u
            row = pl.ds(p, 1)
            wx_ref[u] = node_weight(px_ref[row, :] - ix) * g_ref[row, :]
            y = py_ref[row, :] - iy
            wy = (node_weight(y), node_weight(y - 8.0))
            for i in range(WX):
                wxi = wx_ref[u, i : i + 1, :]
                for h in range(2):
                    acc[2 * i + h] = acc[2 * i + h] + wxi * wy[h]
        return tuple(acc)

    acc = lax.fori_loop(0, LANES // 4, over_p, (jnp.zeros((8, LANES), f32),) * 16)
    for i in range(16):
        nodes_ref[8 * i : 8 * i + 8, :] = acc[i]


def split(x):
    hi = x.astype(bf16)
    return hi, (x - hi.astype(f32)).astype(bf16)


def dot3(x, m_hi, m_lo):
    hi, lo = split(x)
    n = x.shape[0]
    both = dot(jnp.concatenate([hi, lo], axis=0), m_hi)
    return both[:n] + (both[n:] + dot(hi, m_lo))


def dot(a, b):
    return jnp.dot(a, b, preferred_element_type=f32)


@functools.cache
def fourier_tables():
    n1, n2 = 2 * WX - 1, 2 * WY - 1
    size = n1 * n2
    u = np.arange(n1)
    v = np.arange(n2)
    di = np.where(u < WX, u, u - n1)
    dj = np.where(v < WY, v, v - n2)
    DI, DJ = [t.reshape(-1).astype(np.float64) for t in np.meshgrid(di, dj, indexing="ij")]
    k1, k2 = [t.reshape(-1) for t in np.meshgrid(u, v, indexing="ij")]
    keep = [0]
    for m in range(1, size):
        mirror = ((-k1[m]) % n1) * n2 + ((-k2[m]) % n2)
        if m < mirror:
            keep.append(m)
    f1, f2 = k1[keep].astype(np.float64), k2[keep].astype(np.float64)
    nf = len(keep)

    def phase(i, j):
        return 2 * np.pi * (np.outer(i, f1) / n1 + np.outer(j, f2) / n2)

    forward = np.zeros((512, 512))
    p = phase(DI, DJ)
    forward[:size, :nf] = np.cos(p)
    forward[:size, 256 : 256 + nf] = -np.sin(p)
    node = np.arange(WX * WY)
    q = phase(node // WY, node % WY)
    gamma = np.zeros((128, 512))
    gamma[:, :nf] = np.cos(q)
    gamma[:, 256 : 256 + nf] = -np.sin(q)
    weight = np.full(nf, 2.0 / size)
    weight[0] = 1.0 / size
    inverse = np.zeros((512, 128))
    inverse[:nf] = weight[:, None] * np.cos(q).T
    inverse[256 : 256 + nf] = -weight[:, None] * np.sin(q).T
    lattice = np.zeros((8, 512))
    lattice[0, :size] = DI
    lattice[1, :size] = DJ
    ddx = (node // WY)[:, None] - (node // WY)[None, :]
    ddy = (node % WY)[:, None] - (node % WY)[None, :]
    w = biot_factor / (ddx * ddx + ddy * ddy + 1.0)
    own = np.concatenate([(-ddy * w).T, (ddx * w).T], axis=1)

    def halves(x):
        hi = x.astype(np.float32).astype(bf16)
        lo = (x - hi.astype(np.float64)).astype(np.float32).astype(bf16)
        return np.stack([hi, lo])

    return halves(forward), halves(gamma), halves(inverse), lattice.astype(np.float32), halves(own)


def vspec():
    return pl.BlockSpec(memory_space=pltpu.VMEM)


def sspec():
    return pl.BlockSpec(memory_space=pltpu.SMEM)


def tile():
    return pltpu.VMEM((LANES, LANES), f32)


def tiles(n):
    return pltpu.VMEM((n, LANES, LANES), f32)


def one_sided_lanes(a_refs, b_refs, on_a, chunks=2):
    xa_ref, ya_ref = a_refs
    xb_ref, yb_ref, gb_ref = b_refs
    ua_ref, va_ref = on_a
    zero = jnp.zeros((8, LANES), f32)

    def over_a(ia, carry):
        a0 = pl.multiple_of(ia * 8, 8)

        def over_b(chunk, u, acc):
            acc = list(acc)
            rows = pl.ds(pl.multiple_of(chunk * 64 + u * 8, 8), 8)
            xb, yb, gb = xb_ref[rows, :], yb_ref[rows, :], gb_ref[rows, :]
            for r in range(8):
                row = pl.ds(a0 + r, 1)
                dx = xa_ref[row, :] - xb
                dy = ya_ref[row, :] - yb
                w = gb * recip(dx * dx + (dy * dy + 1.0))
                acc[r] = acc[r] + dy * w
                acc[8 + r] = acc[8 + r] + dx * w
            return tuple(acc)

        def over_chunk(chunk, acc):
            for u in range(8):
                acc = over_b(chunk, u, acc)
            return acc

        acc = lax.fori_loop(0, chunks, over_chunk, (zero,) * 16)
        for r in range(8):
            ua_ref[pl.ds(a0 + r, 1), :] = jnp.sum(acc[r], axis=0, keepdims=True)
            va_ref[pl.ds(a0 + r, 1), :] = jnp.sum(acc[8 + r], axis=0, keepdims=True)
        return carry

    lax.fori_loop(0, 16, over_a, 0)


def onehot(condition):
    return jnp.where(condition, 1.0, 0.0).astype(bf16)


def dot_exact(hot, x):
    hi, rest = split(x)[0], None
    rest = x - hi.astype(f32)
    mid, lo = split(rest)
    return (dot(hot, hi) + dot(hot, mid)) + dot(hot, lo)


def dot_near(hot, x):
    hi, lo = split(x)
    return dot(hot, hi) + dot(hot, lo)


def places(index_row):
    n = index_row.shape[1]
    return onehot(lax.broadcasted_iota(jnp.int32, (n, n), 0) == index_row)


def spread_rows(index_row, x):
    return dot_near(places(index_row), x)


def pick_columns(x, hot):
    hi = x.astype(bf16)
    mid, lo = split(x - hi.astype(f32))
    return (dot(hi, hot) + dot(mid, hot)) + dot(lo, hot)


def spread_columns(x, hot):
    dims = (((1,), (1,)), ((), ()))
    hi, lo = split(x)
    return lax.dot_general(hi, hot, dims, preferred_element_type=f32) + lax.dot_general(
        lo, hot, dims, preferred_element_type=f32
    )


def earlier(n):
    return onehot(lax.broadcasted_iota(jnp.int32, (n, n), 0) < lax.broadcasted_iota(jnp.int32, (n, n), 1))


def sort_lists(ints_ref, outbox):
    groups = outbox.shape[0]
    n = ints_ref.shape[1]
    before = earlier(n)
    rows8 = lax.broadcasted_iota(jnp.int32, (8, n), 0)
    slots = lax.broadcasted_iota(jnp.int32, (n, n), 0)
    k = lax.broadcasted_iota(jnp.int32, (1, n), 1)
    outbox[...] = jnp.zeros_like(outbox)
    for step in range(STEPS):
        target = ints_ref[4 + step : 5 + step, :]
        source = ints_ref[6 + step : 7 + step, :]
        owner = lax.shift_right_logical(source, n.bit_length() - 1)
        key = jnp.where(k < ints_ref[8 + step : 9 + step, :], owner, groups)
        row = jnp.bitwise_and(source, n - 1)
        mine = jnp.where(rows8 == key, 1.0, 0.0)
        place = jnp.sum(mine * dot(mine.astype(bf16), before), axis=0, keepdims=True).astype(jnp.int32)
        values = jnp.where(rows8 == 0, target, jnp.where(rows8 == 1, row, 0))
        values = values.astype(f32).astype(bf16)
        count = jnp.sum(mine, axis=1, keepdims=True).astype(jnp.int32)
        for b in range(groups):
            hot = onehot((slots == place) & (key == b))
            found = lax.dot_general(values, hot, (((1,), (1,)), ((), ())), preferred_element_type=f32)
            outbox[b, 2 * step : 2 * step + 2, :] = found[0:2, :].astype(jnp.int32)
            outbox[b, 4 + step : 5 + step, :] = jnp.broadcast_to(count[b : b + 1, :], (1, n))


class Ring:
    def __init__(self, block, own, up, down, part, chunk, send_sem, recv_sem):
        start, size, first = chunk
        self.block = part(block, start, size)
        view = lambda ref: lambda member: part(ref, start, size, member)
        self.own, self.up, self.down = view(own), view(up), view(down)
        self.halves = (
            lambda member: part(own, start, first, member),
            lambda member: part(own, start + first, size - first, member),
        )
        self.send_sem, self.recv_sem = send_sem, recv_sem
        self.grp = lax.axis_index("grp")
        groups = lax.axis_size("grp")
        self.right = lax.rem(self.grp + 1, groups)
        self.left = lax.rem(self.grp + groups - 1, groups)
        self.across = lax.rem(self.grp + 2, groups)
        strip, strips = lax.axis_index("strip"), lax.axis_size("strip")
        self.above = lax.rem(strip + 1, strips)
        self.below = lax.rem(strip + strips - 1, strips)
        self.sent = []

    def send(self, src, dst, device, slot):
        copy = pltpu.make_async_remote_copy(
            src_ref=src,
            dst_ref=dst,
            send_sem=self.send_sem.at[slot],
            recv_sem=self.recv_sem.at[slot],
            device_id=device,
        )
        copy.start()
        self.sent.append(copy)
        return copy

    def to_strips(self, src, member, slot):
        return [
            self.send(src, self.down(member), {"strip": self.above}, slot),
            self.send(src, self.up(member), {"strip": self.below}, slot + 1),
        ]

    def first(self):
        self.from_left = self.send(self.block, self.own(self.grp), {"grp": self.right}, 0)
        self.from_right = self.send(self.block, self.own(self.grp), {"grp": self.left}, 1)
        self.last = self.to_strips(self.block, self.grp, 2)

    def second(self):
        self.from_left.wait_recv()
        half = self.halves[0](self.left)
        self.half_a = self.send(half, half, {"grp": self.right}, 4)
        self.last += self.to_strips(self.own(self.left), self.left, 5)
        self.from_right.wait_recv()
        half = self.halves[1](self.right)
        self.half_b = self.send(half, half, {"grp": self.left}, 7)
        self.last += self.to_strips(self.own(self.right), self.right, 8)

    def third(self):
        self.half_a.wait_recv()
        self.half_b.wait_recv()
        self.last += self.to_strips(self.own(self.across), self.across, 10)

    def finish(self):
        for copy in self.last:
            copy.wait_recv()
        for copy in self.sent:
            copy.wait_send()


class Rings:
    def __init__(self, block, own, up, down, part, chunks, send_sem, recv_sem):
        self.rings = [
            Ring(block, own, up, down, part, chunk, send_sem.at[i], recv_sem.at[i]) for i, chunk in enumerate(chunks)
        ]

    def first(self):
        for ring in self.rings:
            ring.first()

    def second(self):
        for ring in self.rings:
            ring.second()

    def third(self):
        for ring in self.rings:
            ring.third()

    def finish(self):
        for ring in self.rings:
            ring.finish()


def local_kernel(
    offset_in,
    gamma_in,
    anchor_in,
    ints_ref,
    state_ref,
    vel_ref,
    lists_ref,
    up_ref,
    down_ref,
    own_ref,
    offset_ref,
    gamma_ref,
    anchor_ref,
    outbox,
    turned,
    pa,
    pb,
    oa,
    ob,
    load_sem,
    send_sem,
    recv_sem,
    list_send,
    list_recv,
):
    loaded = load_tables([(offset_in, offset_ref), (gamma_in, gamma_ref), (anchor_in, anchor_ref)], load_sem)
    leaves = gamma_ref.shape[0]
    blocks = range(leaves // LANES)
    part = lambda ref, start, size, *member: ref.at[(*member, slice(None), pl.ds(start, size))]
    cut = leaves // 2
    chunks = [(0, cut, cut // 2), (cut, cut, cut // 2)]
    rings = Rings(state_ref, own_ref, up_ref, down_ref, part, chunks, send_sem, recv_sem)
    ring = rings.rings[0]
    groups = lists_ref.shape[0]
    barrier = pltpu.get_barrier_semaphore()
    for device in ({"grp": ring.left}, {"grp": ring.right}, {"strip": ring.above}):
        pl.semaphore_signal(barrier, inc=1, device_id=device)
    for j in range(groups):
        pl.semaphore_signal(barrier, inc=1, device_id={"strip": ring.below, "grp": j})
    loaded()
    for h in blocks:
        rows = pl.ds(h * LANES, LANES)
        for c in range(2):
            column = jnp.broadcast_to(anchor_ref[c : c + 1, h * LANES : (h + 1) * LANES], (LANES, LANES)).T
            state_ref[c, rows, :] = offset_ref[rows, c, :] + column
        state_ref[2, rows, :] = gamma_ref[rows, :]
    pl.semaphore_wait(barrier, 3 + groups)
    rings.first()
    sort_lists(ints_ref, outbox)
    mail = []
    for j in range(groups):
        peer = lax.rem(ring.grp + j, groups)
        copy = pltpu.make_async_remote_copy(
            src_ref=outbox.at[peer],
            dst_ref=lists_ref.at[ring.grp],
            send_sem=list_send.at[j],
            recv_sem=list_recv.at[j],
            device_id={"strip": ring.above, "grp": peer},
        )
        copy.start()
        mail.append(copy)

    for h in blocks:
        rows = pl.ds(h * LANES, LANES)
        for c in range(3):
            turned[h, c] = state_ref[c, rows, :].T
    views = lambda ref, h, n: [ref.at[h, c] for c in range(n)]
    for h in blocks:
        one_sided_lanes(views(turned, h, 2), views(turned, h, 3), views(vel_ref, h, 2))
        rings.rings[h].second()
    first = ints_ref[0:1, :]
    hot_a = places(first)
    hot_b = places(jnp.bitwise_and(first + ints_ref[2:3, :], leaves - 1))
    for c in range(3):
        whole = jnp.concatenate([turned[h, c] for h in blocks], axis=1)
        for ref, hot in ((pa, hot_a), (pb, hot_b)):
            picked = pick_columns(whole, hot)
            for h in blocks:
                ref[h, c] = picked[:, h * LANES : (h + 1) * LANES]
    for h in blocks:
        between = rings.third if h == 0 else lambda: None
        mutual_lanes(views(pa, h, 3), views(pb, h, 3), views(oa, h, 2), views(ob, h, 2), between)
    for c, sign in ((0, -biot_factor), (1, biot_factor)):
        on_a, on_b = [jnp.concatenate([ref[h, c] for h in blocks], axis=1) for ref in (oa, ob)]
        pairs = spread_columns(on_a, hot_a) - spread_columns(on_b, hot_b)
        for h in blocks:
            vel_ref[h, c] = (vel_ref[h, c] + pairs[:, h * LANES : (h + 1) * LANES]) * sign
    rings.finish()
    for copy in mail:
        copy.wait()


def walk(ints_ref, lists_ref, leaves, step, visit):
    live = ints_ref[8 + step, 0]
    shift = leaves.bit_length() - 1

    def mine(k):
        source = ints_ref[6 + step, k]
        block, row = lax.shift_right_logical(source, shift), jnp.bitwise_and(source, leaves - 1)
        visit(k, jnp.where(k < live, ints_ref[4 + step, k], leaves), 0, block, row)

    loop8(live, mine)
    base = live
    for g in range(lists_ref.shape[0]):
        count = lists_ref[g, 4 + step, 0]

        def theirs(k, g=g, base=base, count=count):
            leaf = jnp.where(k < count, lists_ref[g, 2 * step + 1, k], leaves)
            visit(base + k, leaf, 1, g, lists_ref[g, 2 * step, k])

        loop8(count, theirs)
        base = base + count
    return base


def cross_kernel(state_ref, up_ref, down_ref, ints_ref, lists_ref, vel_ref, ra, rb, ta, tb, oa, total_ref):
    leaves = state_ref.shape[1]
    sides = (up_ref, down_ref)
    total_ref[...] = jnp.zeros_like(total_ref)

    def fetch(n, leaf, side, block, row):
        own = jnp.minimum(leaf, leaves - 1)
        for c in range(2):
            ra[c, pl.ds(n, 1), :] = state_ref[c, pl.ds(own, 1), :]
        for c in range(3):
            rb[c, pl.ds(n, 1), :] = sides[side][block, c, pl.ds(row, 1), :]

    total = walk(ints_ref, lists_ref, leaves, 0, fetch)

    def pair_group(i, carry):
        rows = pl.ds(pl.multiple_of(i * LANES, LANES), LANES)
        half = LANES // 2
        few = total - i * LANES <= half

        @pl.when(few)
        def _():
            low = pl.ds(pl.multiple_of(i * LANES, LANES), half)
            high = pl.ds(pl.multiple_of(i * LANES + half, half), half)
            for c in range(2):
                ra[c, high, :] = ra[c, low, :]
            for c in range(3):
                rb[c, high, :] = pltpu.roll(rb[c, low, :], half, 1)

        for c in range(2):
            ta[c] = ra[c, rows, :].T
        for c in range(3):
            tb[c] = rb[c, rows, :].T
        one_sided_lanes(
            [ta.at[c] for c in range(2)],
            [tb.at[c] for c in range(3)],
            [oa.at[c] for c in range(2)],
            jnp.where(few, 1, 2),
        )
        for c, sign in ((0, -biot_factor), (1, biot_factor)):
            found = oa[c].T * sign
            ra[c, rows, :] = found
            ra[c, pl.ds(pl.multiple_of(i * LANES, LANES), half), :] = found[:half] + jnp.where(few, found[half:], 0.0)
        return carry

    lax.fori_loop(0, (total + LANES - 1) // LANES, pair_group, 0)

    def spread(n, leaf, side, block, row):
        for c in range(2):
            total_ref[c, pl.ds(leaf, 1), :] += ra[c, pl.ds(n, 1), :]

    walk(ints_ref, lists_ref, leaves, 0, spread)
    for c in range(2):
        vel_ref[c] = total_ref[c, pl.ds(0, leaves), :]


def lattice_waves(x, y, lat, fwd):
    n = x.shape[0]
    x = jnp.concatenate([x] * 4, axis=1) + lat[0:1, :]
    y = jnp.concatenate([y] * 4, axis=1) + lat[1:2, :]
    w = biot_factor * recip(x * x + y * y + 1.0)
    waves = dot3(jnp.concatenate([-y * w, x * w], axis=0), fwd[0], fwd[1])
    return waves[:n], waves[n:]


def wave_product(k, g, sign):
    kr, ki, gr, gi = k[:, :256], k[:, 256:], g[:, :256], g[:, 256:]
    if sign < 0:
        return jnp.concatenate([kr * gr + ki * gi, kr * gi - ki * gr], axis=1)
    return jnp.concatenate([kr * gr - ki * gi, kr * gi + ki * gr], axis=1)


def load_tables(pairs, sem):
    copies = [pltpu.make_async_copy(src, dst, sem.at[i]) for i, (src, dst) in enumerate(pairs)]
    for copy in copies:
        copy.start()

    def wait():
        for copy in copies:
            copy.wait()

    return wait


def spread_anchors(anchor_ref, half):
    cols = slice(half * LANES, (half + 1) * LANES)
    part = [jnp.broadcast_to(anchor_ref[c : c + 1, cols], (LANES // 4, LANES)) for c in range(2)]
    return jnp.concatenate(part + part, axis=0).T


def cross_waves(
    spread_ref,
    up_ref,
    down_ref,
    vel_in_ref,
    ints_ref,
    lists_ref,
    fwd_in,
    gam_in,
    inv_in,
    lat,
    vel_ref,
    rb,
    rd,
    ra,
    total_ref,
    far_anc,
    fwd,
    gam,
    inv,
    sem,
):
    leaves = vel_in_ref.shape[1]
    sides = (up_ref, down_ref)
    ready = load_tables([(fwd_in, fwd), (gam_in, gam), (inv_in, inv)], sem)
    quarter = LANES // 4
    for side in range(2):
        for b in range(up_ref.shape[0]):
            lines = [
                jnp.broadcast_to(sides[side][b, leaves + q : leaves + q + 1, :], (quarter, LANES)) for q in range(4)
            ]
            anchors = jnp.concatenate(lines, axis=0).T
            far_anc[side, b, pl.ds(0, LANES, stride=2), :] = anchors
            far_anc[side, b, pl.ds(1, LANES, stride=2), :] = pltpu.roll(anchors, LANES // 2, 1)
    for c in range(2):
        total_ref[c, pl.ds(0, leaves), :] = vel_in_ref[c]

    def fetch(n, leaf, side, block, row):
        rb[pl.ds(n, 1), :] = sides[side][block, pl.ds(row, 1), :]
        own = jnp.minimum(leaf, leaves - 1)
        rd[pl.ds(n, 1), :] = spread_ref[pl.ds(own, 1), :] - far_anc[side, block, pl.ds(row, 1), :]

    total = walk(ints_ref, lists_ref, leaves, 1, fetch)
    ready()

    def pair_group(i, carry):
        rows = pl.ds(pl.multiple_of(i * LANES, LANES), LANES)
        waves = dot3(rb[rows, :], gam[0], gam[1])
        gap = rd[rows, :]
        x = jnp.broadcast_to(gap[:, 0:1], (LANES, LANES))
        y = jnp.broadcast_to(gap[:, quarter : quarter + 1], (LANES, LANES))
        products = [wave_product(k, waves, 1) for k in lattice_waves(x, y, lat, fwd)]
        found = dot3(jnp.concatenate(products, axis=0), inv[0], inv[1])
        ra[0, rows, :] = found[:LANES]
        ra[1, rows, :] = found[LANES:]
        return carry

    lax.fori_loop(0, (total + LANES - 1) // LANES, pair_group, 0)

    def spread(n, leaf, side, block, row):
        for c in range(2):
            total_ref[c, pl.ds(leaf, 1), :] += ra[c, pl.ds(n, 1), :]

    walk(ints_ref, lists_ref, leaves, 1, spread)
    for c in range(2):
        vel_ref[c] = total_ref[c, pl.ds(0, leaves), :]


def regroup_kernel(step, *refs):
    last = step == STEPS - 1
    refs = list(refs)
    take = lambda n: [refs.pop(0) for _ in range(n)]
    vel_ref, shift_ref, g_ref, anchor_ref, dest_ref = take(5)
    leaves = vel_ref.shape[1]
    if not last:
        turned_ref, ints_ref, list_ref, fwd_in, gam_in, inv_in, lat, own_in = take(8)
        block, spread_ref, next_vel, up_ref, down_ref = take(5)
    else:
        gamma_ref, final_ref = take(2)
    px, py, pg, wx, out, nodes, outbox, box_ref, send_sem, recv_sem, own_sem = take(11)
    if not last:
        own_ref, ra, rb, rd, fwd, gam, inv, own, ring_send, ring_recv, table_sem = take(11)
        ready = load_tables([(fwd_in, fwd), (gam_in, gam), (inv_in, inv), (own_in, own)], table_sem)
    else:
        (spread_ref,) = take(1)
    if not last:
        part = lambda ref, start, size, *member: ref.at[(*member, pl.ds(start, size))]
        cut = leaves // 2
        chunks = [(0, cut, cut // 2), (cut, cut + 8, cut // 2)]
        rings = Rings(block, own_ref, up_ref, down_ref, part, chunks, ring_send, ring_recv)
        ring = rings.rings[0]
    strip = lax.axis_index("strip")
    strips = outbox.shape[0]
    barrier = pltpu.get_barrier_semaphore()

    def greet(d, carry):
        pl.semaphore_signal(barrier, inc=1, device_id={"strip": jnp.bitwise_and(strip + d, strips - 1)})
        return carry

    lax.fori_loop(1, strips, greet, 0, unroll=8)
    if not last:
        for device in ({"grp": ring.left}, {"grp": ring.right}):
            pl.semaphore_signal(barrier, inc=1, device_id=device)

    def remesh(i, carry):
        rows = pl.ds(pl.multiple_of(i * LANES, LANES), LANES)
        for c, dst in ((0, px), (1, py)):
            if last:
                node = lax.broadcasted_iota(jnp.int32, (LANES, LANES), 0)
                node = jnp.bitwise_and(node, WY - 1) if c else lax.shift_right_logical(node, WY.bit_length() - 1)
                dst[...] = node.astype(f32) + (time_step * vel_ref[c, rows, :]).T
            else:
                moved = (shift_ref[rows, c, :] + time_step * vel_ref[c, rows, :]).T
                dst[...] = moved + time_step * turned_ref[i, c]
        pg[...] = g_ref[rows, :].T
        remesh_lanes(px, py, pg, wx, out)
        nodes[rows, :] = out[...].T
        return carry

    lax.fori_loop(0, leaves // LANES, remesh, 0)
    dest = dest_ref[step]
    named = jnp.where(lax.broadcasted_iota(jnp.int32, (strips, leaves), 0) == dest, 1.0, 0.0)
    rank = jnp.sum(named * dot(named.astype(bf16), earlier(leaves)), axis=0, keepdims=True)
    hot = [onehot(jnp.where(rank == float(r), named, 0.0) > 0.5) for r in range(2)]
    for r in range(2):
        outbox[:, r, :] = dot_exact(hot[r], nodes[...])
    lane = lax.broadcasted_iota(jnp.int32, (strips, LANES), 1)
    if last:
        spread = anchor_ref[...]
    else:
        spread = jnp.concatenate([spread_anchors(anchor_ref, h) for h in range(leaves // LANES)], axis=0)
    anchors = [dot_exact(hot[r], spread) for r in range(2)]
    outbox[:, 2, :] = jnp.where(lane < LANES // 2, anchors[0], anchors[1])
    pl.semaphore_wait(barrier, strips - 1 + (0 if last else 2))

    def send(d, carry):
        to = jnp.bitwise_and(strip + d, strips - 1)
        pltpu.make_async_remote_copy(
            src_ref=outbox.at[to],
            dst_ref=box_ref.at[strip],
            send_sem=send_sem,
            recv_sem=recv_sem,
            device_id={"strip": to},
        ).start()
        return carry

    lax.fori_loop(1, strips, send, 0, unroll=8)
    mine = pltpu.make_async_copy(outbox.at[strip], box_ref.at[strip], own_sem)
    mine.start()
    mine.wait()
    rest = pl.ds(0, strips - 1)
    pltpu.make_async_copy(box_ref.at[rest], box_ref.at[rest], recv_sem).wait()
    pltpu.make_async_copy(outbox.at[rest], outbox.at[rest], send_sem).wait()
    anchors = box_ref[:, 2, :]
    rolled = pltpu.roll(anchors, LANES // 2, 1)
    if last:
        for r in range(2):
            gamma_ref[pl.ds(r, strips, stride=2), :] = box_ref[:, r, :]
        spread_ref[pl.ds(0, strips, stride=2), :] = anchors
        spread_ref[pl.ds(1, strips, stride=2), :] = rolled
        for h in range(leaves // LANES):
            turned = spread_ref[pl.ds(h * LANES, LANES), :].T
            for c in range(2):
                row = turned[c * (LANES // 4) : c * (LANES // 4) + 1, :]
                final_ref[c : c + 1, h * LANES : (h + 1) * LANES] = row
        return
    for r in range(2):
        block[pl.ds(r, strips, stride=2), :] = box_ref[:, r, :]
    turned = anchors.T
    for q in range(4):
        block[leaves + q : leaves + q + 1, :] = turned[q * (LANES // 4) : q * (LANES // 4) + 1, :]
    block[leaves + 4 : leaves + 8, :] = jnp.zeros((4, LANES), f32)
    rings.first()
    spread_ref[pl.ds(0, strips, stride=2), :] = jnp.where(lane < LANES // 2, anchors, rolled)
    spread_ref[pl.ds(1, strips, stride=2), :] = jnp.where(lane < LANES // 2, rolled, anchors)
    ready()
    field = dot3(block[pl.ds(0, leaves), :], own[0], own[1])

    def pair_group(i, between):
        base = i * LANES

        def fetch(k):
            start = list_ref[1, base + k]
            first = pl.ds(start, 1)
            second = pl.ds(jnp.bitwise_and(start + list_ref[3, base + k], leaves - 1), 1)
            row = pl.ds(base + k, 1)
            ra[0, row, :] = block[first, :]
            rb[0, row, :] = block[second, :]
            rd[row, :] = spread_ref[first, :] - spread_ref[second, :]

        loop8(LANES, fetch)
        between()
        rows = pl.ds(base, LANES)
        gap = rd[rows, :]
        x = jnp.broadcast_to(gap[:, 0:1], (LANES, LANES))
        y = jnp.broadcast_to(gap[:, LANES // 4 : LANES // 4 + 1], (LANES, LANES))
        waves = dot3(jnp.concatenate([ra[0, rows, :], rb[0, rows, :]], axis=0), gam[0], gam[1])
        wa, wb = waves[:LANES], waves[LANES:]
        kernels = lattice_waves(x, y, lat, fwd)
        products = [wave_product(k, wb, 1) for k in kernels] + [wave_product(k, wa, -1) for k in kernels]
        found = dot3(jnp.concatenate(products, axis=0), inv[0], inv[1])
        for c in range(2):
            ra[c, rows, :] = found[c * LANES : (c + 1) * LANES]
            rb[c, rows, :] = found[(2 + c) * LANES : (3 + c) * LANES]

    for i in range(leaves // LANES):
        pair_group(i, (rings.second, rings.third)[i] if i < 2 else lambda: None)
    first = ints_ref[1:2, :]
    second = jnp.bitwise_and(first + ints_ref[3:4, :], leaves - 1)
    for c in range(2):
        next_vel[c] = (
            field[:, c * LANES : (c + 1) * LANES]
            + spread_rows(first, ra[c])
            - spread_rows(second, rb[c])
        )
    rings.finish()


def shape(*sizes, dtype=f32):
    return jax.ShapeDtypeStruct(sizes, dtype)


def anywhere():
    return pl.BlockSpec(memory_space=pl.ANY)


def call(kernel, out_shape, in_specs, out_specs, scratch, vmem=48, **kw):
    return pl.pallas_call(
        kernel,
        out_shape=out_shape,
        in_specs=in_specs,
        out_specs=out_specs,
        scratch_shapes=scratch,
        compiler_params=pltpu.CompilerParams(vmem_limit_bytes=vmem * 2**20, **kw),
    )


def run_local(offsets, gamma, anchor, ints):
    leaves = gamma.shape[0]
    groups = lax.axis_size("grp")
    state = (3, leaves, LANES)
    wide = (groups,) + state
    dma = pltpu.SemaphoreType.DMA
    cols = lambda n: pltpu.VMEM((leaves // LANES, n, LANES, LANES), f32)
    return call(
        local_kernel,
        (shape(*state), shape(leaves // LANES, 2, LANES, LANES), shape(groups, 8, leaves, dtype=jnp.int32)) + (shape(*wide),) * 3,
        [pl.BlockSpec(memory_space=pltpu.HBM)] * 3 + [vspec()],
        (vspec(),) * 3 + (anywhere(),) * 3,
        [pltpu.VMEM(offsets.shape, f32), pltpu.VMEM(gamma.shape, f32), pltpu.VMEM(anchor.shape, f32)]
        + [pltpu.VMEM((groups, 8, leaves), jnp.int32), cols(3), cols(3), cols(3), cols(2), cols(2)]
        + [dma((3,)), dma((2, 12)), dma((2, 12)), dma((groups,)), dma((groups,))],
        collective_id=0,
        has_side_effects=True,
    )(offsets, gamma, anchor, ints)[:5]


def run_cross(state, up, down, ints, lists):
    leaves = state.shape[1]
    most = (1 + up.shape[0]) * leaves + LANES
    return call(
        cross_kernel,
        shape(2, leaves, LANES),
        [vspec()] * 3 + [sspec()] * 2,
        vspec(),
        [pltpu.VMEM((2, most, LANES), f32), pltpu.VMEM((3, most, LANES), f32), tiles(2), tiles(3), tiles(2)]
        + [pltpu.VMEM((2, leaves + 8, LANES), f32)],
    )(state, up, down, ints, lists)


def run_cross_waves(spread, up, down, vel, ints, lists, tables):
    leaves = vel.shape[1]
    groups = up.shape[0]
    most = (1 + groups) * leaves + 8
    fwd, gam, inv, lat, own = tables
    return call(
        cross_waves,
        shape(*vel.shape),
        [vspec()] * 4 + [sspec()] * 2 + [anywhere()] * 3 + [vspec()],
        vspec(),
        [pltpu.VMEM((most, LANES), f32), pltpu.VMEM((most, LANES), f32), pltpu.VMEM((2, most, LANES), f32)]
        + [pltpu.VMEM((2, leaves + 8, LANES), f32), pltpu.VMEM((2, groups, leaves, LANES), f32)]
        + [pltpu.VMEM(t.shape, bf16) for t in (fwd, gam, inv)]
        + [pltpu.SemaphoreType.DMA((3,))],
    )(spread, up, down, vel, ints, lists, fwd, gam, inv, lat)


def run_regroup(step, vel, shifted, gamma, anchor, dest, *more):
    last = step == STEPS - 1
    leaves = vel.shape[1]
    groups, strips = lax.axis_size("grp"), lax.axis_size("strip")
    dma = pltpu.SemaphoreType.DMA
    box = (strips, 3, LANES)
    in_specs = [vspec()] * 5
    scratch = [tile(), tile(), tile(), pltpu.VMEM((4, WX, LANES), f32), tile(), pltpu.VMEM((leaves, LANES), f32)]
    scratch += [pltpu.VMEM(box, f32), pltpu.VMEM(box, f32), dma, dma, dma]
    if last:
        out_shape = [shape(leaves, LANES), shape(2, leaves)]
        scratch += [pltpu.VMEM((leaves, LANES), f32)]
    else:
        block = (leaves + 8, LANES)
        wide = (groups,) + block
        out_shape = [shape(*block), shape(leaves, LANES), shape(2, leaves, LANES), shape(*wide), shape(*wide)]
        in_specs += [vspec(), vspec(), sspec()] + [anywhere()] * 3 + [vspec(), anywhere()]
        rows = lambda n: pltpu.VMEM((n, leaves, LANES), f32)
        scratch += [pltpu.VMEM(wide, f32), rows(2), rows(2), pltpu.VMEM((leaves, LANES), f32)]
        scratch += [pltpu.VMEM(more[i].shape, bf16) for i in (3, 4, 5, 7)]
        scratch += [dma((2, 12)), dma((2, 12)), dma((4,))]
    return call(
        functools.partial(regroup_kernel, step),
        tuple(out_shape),
        in_specs,
        (vspec(),) * len(out_shape),
        scratch,
        collective_id=1 + step,
        has_side_effects=True,
    )(vel, shifted, gamma, anchor, dest, *more)


def on_device(
    offsets,
    circulation,
    window_anchor,
    local_first,
    local_offset,
    cross_target,
    cross_source,
    cross_count,
    destination,
):
    anchor = window_anchor.T
    dest = destination.transpose(0, 2, 1)
    live = jnp.broadcast_to(cross_count, local_first.shape)
    ints = jnp.concatenate([local_first, local_offset, cross_target, cross_source, live, live, live, live], axis=0)
    tables = [jnp.asarray(t) for t in fourier_tables()]
    state, turned, inbox, up, down = run_local(offsets, circulation, anchor, ints)
    vel = run_cross(state, up, down, ints, inbox)
    block, spread, vel, up, down = run_regroup(
        0, vel, offsets, circulation, anchor, dest, turned, ints, ints, *tables
    )
    vel = run_cross_waves(spread, up, down, vel, ints, inbox, tables)
    gamma, anchor = run_regroup(1, vel, block, block, spread, dest)
    return gamma, anchor.T


def solution(mesh):
    rows = P(("strip", "grp"))
    lists = P(None, ("strip", "grp"))
    return jax.shard_map(
        on_device,
        mesh=mesh,
        in_specs=(rows, rows, rows, lists, lists, lists, lists, lists, lists),
        out_specs=(rows, rows),
        check_vma=False,
    )
```

```python
import functools
import jax
import jax.numpy as jnp
import numpy as np
from jax import lax
from jax.experimental import pallas as pl
from jax.experimental.pallas import tpu as pltpu
from jax.sharding import PartitionSpec as P

WX = 8
WY = 16
STEPS = 2
time_step = 0.5
biot_factor = 0.15915494309189535
LANES = 128
f32 = jnp.float32
bf16 = jnp.bfloat16


def recip(x):
    return pl.reciprocal(x, approx=True)


def mutual_lanes(a_refs, b_refs, on_a, on_b, between):
    xa_ref, ya_ref, ga_ref = a_refs
    xb_ref, yb_ref, gb_ref = b_refs
    ua_ref, va_ref = on_a
    ub_ref, vb_ref = on_b
    ub_ref[...] = jnp.zeros_like(ub_ref)
    vb_ref[...] = jnp.zeros_like(vb_ref)
    zero = jnp.zeros((8, LANES), f32)

    def over_a(ia, carry):
        a0 = pl.multiple_of(ia * 8, 8)

        def over_b(ib, acc):
            acc = list(acc)
            rows = pl.ds(pl.multiple_of(ib * 8, 8), 8)
            xb, yb, gb = xb_ref[rows, :], yb_ref[rows, :], gb_ref[rows, :]
            ub, vb = ub_ref[rows, :], vb_ref[rows, :]
            for r in range(8):
                row = pl.ds(a0 + r, 1)
                dx = xa_ref[row, :] - xb
                dy = ya_ref[row, :] - yb
                w = recip(dx * dx + dy * dy + 1.0)
                tx = dx * w
                ty = dy * w
                acc[r] = acc[r] + gb * ty
                acc[8 + r] = acc[8 + r] + gb * tx
                ga = ga_ref[row, :]
                ub = ub + ga * ty
                vb = vb + ga * tx
            ub_ref[rows, :] = ub
            vb_ref[rows, :] = vb
            return tuple(acc)

        acc = lax.fori_loop(0, 16, over_b, (zero,) * 16, unroll=8)
        for r in range(8):
            ua_ref[pl.ds(a0 + r, 1), :] = jnp.sum(acc[r], axis=0, keepdims=True)
            va_ref[pl.ds(a0 + r, 1), :] = jnp.sum(acc[8 + r], axis=0, keepdims=True)
        return carry

    lax.fori_loop(0, 8, over_a, 0)
    between()
    lax.fori_loop(8, 16, over_a, 0)


def loop8(count, body):
    def eight(k, carry):
        for u in range(8):
            body(k * 8 + u)
        return carry

    lax.fori_loop(0, (count + 7) // 8, eight, 0)


def node_weight(distance):
    r = jnp.abs(distance)
    inner = 1.0 + r * r * (1.5 * r - 2.5)
    s = jnp.maximum(2.0 - r, 0.0)
    outer = (0.5 * s) * s * (1.0 - r)
    return jnp.where(r < 1.0, inner, outer)


def remesh_lanes(px_ref, py_ref, g_ref, wx_ref, nodes_ref):
    ix = lax.broadcasted_iota(jnp.int32, (WX, LANES), 0).astype(f32)
    iy = lax.broadcasted_iota(jnp.int32, (WX, LANES), 0).astype(f32)

    def over_p(p4, acc):
        acc = list(acc)
        for u in range(4):
            p = p4 * 4 + u
            row = pl.ds(p, 1)
            wx_ref[u] = node_weight(px_ref[row, :] - ix) * g_ref[row, :]
            y = py_ref[row, :] - iy
            wy = (node_weight(y), node_weight(y - 8.0))
            for i in range(WX):
                wxi = wx_ref[u, i : i + 1, :]
                for h in range(2):
                    acc[2 * i + h] = acc[2 * i + h] + wxi * wy[h]
        return tuple(acc)

    acc = lax.fori_loop(0, LANES // 4, over_p, (jnp.zeros((8, LANES), f32),) * 16)
    for i in range(16):
        nodes_ref[8 * i : 8 * i + 8, :] = acc[i]


def split(x):
    hi = x.astype(bf16)
    return hi, (x - hi.astype(f32)).astype(bf16)


def dot3(x, m_hi, m_lo):
    hi, lo = split(x)
    n = x.shape[0]
    both = dot(jnp.concatenate([hi, lo], axis=0), m_hi)
    return both[:n] + (both[n:] + dot(hi, m_lo))


def dot(a, b):
    return jnp.dot(a, b, preferred_element_type=f32)


@functools.cache
def fourier_tables():
    n1, n2 = 2 * WX - 1, 2 * WY - 1
    size = n1 * n2
    u = np.arange(n1)
    v = np.arange(n2)
    di = np.where(u < WX, u, u - n1)
    dj = np.where(v < WY, v, v - n2)
    DI, DJ = [t.reshape(-1).astype(np.float64) for t in np.meshgrid(di, dj, indexing="ij")]
    k1, k2 = [t.reshape(-1) for t in np.meshgrid(u, v, indexing="ij")]
    keep = [0]
    for m in range(1, size):
        mirror = ((-k1[m]) % n1) * n2 + ((-k2[m]) % n2)
        if m < mirror:
            keep.append(m)
    f1, f2 = k1[keep].astype(np.float64), k2[keep].astype(np.float64)
    nf = len(keep)

    def phase(i, j):
        return 2 * np.pi * (np.outer(i, f1) / n1 + np.outer(j, f2) / n2)

    forward = np.zeros((512, 512))
    p = phase(DI, DJ)
    forward[:size, :nf] = np.cos(p)
    forward[:size, 256 : 256 + nf] = -np.sin(p)
    node = np.arange(WX * WY)
    q = phase(node // WY, node % WY)
    gamma = np.zeros((128, 512))
    gamma[:, :nf] = np.cos(q)
    gamma[:, 256 : 256 + nf] = -np.sin(q)
    weight = np.full(nf, 2.0 / size)
    weight[0] = 1.0 / size
    inverse = np.zeros((512, 128))
    inverse[:nf] = weight[:, None] * np.cos(q).T
    inverse[256 : 256 + nf] = -weight[:, None] * np.sin(q).T
    lattice = np.zeros((8, 512))
    lattice[0, :size] = DI
    lattice[1, :size] = DJ
    ddx = (node // WY)[:, None] - (node // WY)[None, :]
    ddy = (node % WY)[:, None] - (node % WY)[None, :]
    w = biot_factor / (ddx * ddx + ddy * ddy + 1.0)
    own = np.concatenate([(-ddy * w).T, (ddx * w).T], axis=1)

    def halves(x):
        hi = x.astype(np.float32).astype(bf16)
        lo = (x - hi.astype(np.float64)).astype(np.float32).astype(bf16)
        return np.stack([hi, lo])

    return halves(forward), halves(gamma), halves(inverse), lattice.astype(np.float32), halves(own)


def vspec():
    return pl.BlockSpec(memory_space=pltpu.VMEM)


def sspec():
    return pl.BlockSpec(memory_space=pltpu.SMEM)


def tile():
    return pltpu.VMEM((LANES, LANES), f32)


def tiles(n):
    return pltpu.VMEM((n, LANES, LANES), f32)


def one_sided_lanes(a_refs, b_refs, on_a, chunks=2):
    xa_ref, ya_ref = a_refs
    xb_ref, yb_ref, gb_ref = b_refs
    ua_ref, va_ref = on_a
    zero = jnp.zeros((8, LANES), f32)

    def over_a(ia, carry):
        a0 = pl.multiple_of(ia * 16, 16)

        def over_b(ib, acc):
            acc = list(acc)
            rows = pl.ds(ib * 8, 8)
            xb, yb, gb = xb_ref[rows, :], yb_ref[rows, :], gb_ref[rows, :]
            for r in range(16):
                row = pl.ds(a0 + r, 1)
                dx = xa_ref[row, :] - xb
                dy = ya_ref[row, :] - yb
                w = gb * recip(dx * dx + (dy * dy + 1.0))
                acc[r] = acc[r] + dy * w
                acc[16 + r] = acc[16 + r] + dx * w
            return tuple(acc)

        acc = (zero,) * 32
        for ib in range(8 * chunks):
            acc = over_b(ib, acc)
        for r in range(16):
            ua_ref[pl.ds(a0 + r, 1), :] = jnp.sum(acc[r], axis=0, keepdims=True)
            va_ref[pl.ds(a0 + r, 1), :] = jnp.sum(acc[16 + r], axis=0, keepdims=True)
        return carry

    lax.fori_loop(0, LANES // 16, over_a, 0)


def onehot(condition):
    return jnp.where(condition, 1.0, 0.0).astype(bf16)


def dot_exact(hot, x):
    hi, rest = split(x)[0], None
    rest = x - hi.astype(f32)
    mid, lo = split(rest)
    return (dot(hot, hi) + dot(hot, mid)) + dot(hot, lo)


def dot_near(hot, x):
    hi, lo = split(x)
    return dot(hot, hi) + dot(hot, lo)


def places(index_row):
    n = index_row.shape[1]
    return onehot(lax.broadcasted_iota(jnp.int32, (n, n), 0) == index_row)


def spread_rows(index_row, x):
    return dot_near(places(index_row), x)


def pick_columns(x, hot):
    hi = x.astype(bf16)
    mid, lo = split(x - hi.astype(f32))
    return (dot(hi, hot) + dot(mid, hot)) + dot(lo, hot)


def spread_columns(x, hot):
    dims = (((1,), (1,)), ((), ()))
    hi, lo = split(x)
    return lax.dot_general(hi, hot, dims, preferred_element_type=f32) + lax.dot_general(
        lo, hot, dims, preferred_element_type=f32
    )


def earlier(n):
    return onehot(lax.broadcasted_iota(jnp.int32, (n, n), 0) < lax.broadcasted_iota(jnp.int32, (n, n), 1))


def sort_lists(ints_ref, outbox):
    groups = outbox.shape[0]
    n = ints_ref.shape[1]
    before = earlier(n)
    rows8 = lax.broadcasted_iota(jnp.int32, (8, n), 0)
    slots = lax.broadcasted_iota(jnp.int32, (n, n), 0)
    k = lax.broadcasted_iota(jnp.int32, (1, n), 1)
    outbox[...] = jnp.zeros_like(outbox)
    for step in range(STEPS):
        target = ints_ref[4 + step : 5 + step, :]
        source = ints_ref[6 + step : 7 + step, :]
        owner = lax.shift_right_logical(source, n.bit_length() - 1)
        key = jnp.where(k < ints_ref[8 + step : 9 + step, :], owner, groups)
        row = jnp.bitwise_and(source, n - 1)
        mine = jnp.where(rows8 == key, 1.0, 0.0)
        place = jnp.sum(mine * dot(mine.astype(bf16), before), axis=0, keepdims=True).astype(jnp.int32)
        values = jnp.where(rows8 == 0, target, jnp.where(rows8 == 1, row, 0))
        values = values.astype(f32).astype(bf16)
        count = jnp.sum(mine, axis=1, keepdims=True).astype(jnp.int32)
        for b in range(groups):
            hot = onehot((slots == place) & (key == b))
            found = lax.dot_general(values, hot, (((1,), (1,)), ((), ())), preferred_element_type=f32)
            outbox[b, 2 * step : 2 * step + 2, :] = found[0:2, :].astype(jnp.int32)
            outbox[b, 4 + step : 5 + step, :] = jnp.broadcast_to(count[b : b + 1, :], (1, n))


class Ring:
    def __init__(self, block, own, up, down, part, chunk, send_sem, recv_sem):
        start, size, first = chunk
        self.block = part(block, start, size)
        view = lambda ref: lambda member: part(ref, start, size, member)
        self.own, self.up, self.down = view(own), view(up), view(down)
        self.halves = (
            lambda member: part(own, start, first, member),
            lambda member: part(own, start + first, size - first, member),
        )
        self.send_sem, self.recv_sem = send_sem, recv_sem
        self.grp = lax.axis_index("grp")
        groups = lax.axis_size("grp")
        self.right = lax.rem(self.grp + 1, groups)
        self.left = lax.rem(self.grp + groups - 1, groups)
        self.across = lax.rem(self.grp + 2, groups)
        strip, strips = lax.axis_index("strip"), lax.axis_size("strip")
        self.above = lax.rem(strip + 1, strips)
        self.below = lax.rem(strip + strips - 1, strips)
        self.sent = []

    def send(self, src, dst, device, slot):
        copy = pltpu.make_async_remote_copy(
            src_ref=src,
            dst_ref=dst,
            send_sem=self.send_sem.at[slot],
            recv_sem=self.recv_sem.at[slot],
            device_id=device,
        )
        copy.start()
        self.sent.append(copy)
        return copy

    def to_strips(self, src, member, slot):
        return [
            self.send(src, self.down(member), {"strip": self.above}, slot),
            self.send(src, self.up(member), {"strip": self.below}, slot + 1),
        ]

    def first(self):
        self.from_left = self.send(self.block, self.own(self.grp), {"grp": self.right}, 0)
        self.from_right = self.send(self.block, self.own(self.grp), {"grp": self.left}, 1)
        self.last = self.to_strips(self.block, self.grp, 2)

    def second(self):
        self.from_left.wait_recv()
        half = self.halves[0](self.left)
        self.half_a = self.send(half, half, {"grp": self.right}, 4)
        self.last += self.to_strips(self.own(self.left), self.left, 5)
        self.from_right.wait_recv()
        half = self.halves[1](self.right)
        self.half_b = self.send(half, half, {"grp": self.left}, 7)
        self.last += self.to_strips(self.own(self.right), self.right, 8)

    def third(self):
        self.half_a.wait_recv()
        self.half_b.wait_recv()
        self.last += self.to_strips(self.own(self.across), self.across, 10)

    def finish(self):
        for copy in self.last:
            copy.wait_recv()
        for copy in self.sent:
            copy.wait_send()


class Rings:
    def __init__(self, block, own, up, down, part, chunks, send_sem, recv_sem):
        self.rings = [
            Ring(block, own, up, down, part, chunk, send_sem.at[i], recv_sem.at[i]) for i, chunk in enumerate(chunks)
        ]

    def first(self):
        for ring in self.rings:
            ring.first()

    def second(self):
        for ring in self.rings:
            ring.second()

    def third(self):
        for ring in self.rings:
            ring.third()

    def finish(self):
        for ring in self.rings:
            ring.finish()


def local_kernel(
    offset_in,
    gamma_in,
    anchor_in,
    ints_ref,
    state_ref,
    vel_ref,
    lists_ref,
    up_ref,
    down_ref,
    own_ref,
    offset_ref,
    gamma_ref,
    anchor_ref,
    outbox,
    turned,
    pa,
    pb,
    oa,
    ob,
    load_sem,
    send_sem,
    recv_sem,
    list_send,
    list_recv,
):
    loaded = load_tables([(offset_in, offset_ref), (gamma_in, gamma_ref), (anchor_in, anchor_ref)], load_sem)
    leaves = gamma_ref.shape[0]
    blocks = range(leaves // LANES)
    part = lambda ref, start, size, *member: ref.at[(*member, slice(None), pl.ds(start, size))]
    cut = leaves // 2
    chunks = [(0, cut, cut // 2), (cut, cut, cut // 2)]
    rings = Rings(state_ref, own_ref, up_ref, down_ref, part, chunks, send_sem, recv_sem)
    ring = rings.rings[0]
    groups = lists_ref.shape[0]
    barrier = pltpu.get_barrier_semaphore()
    for device in ({"grp": ring.left}, {"grp": ring.right}, {"strip": ring.above}):
        pl.semaphore_signal(barrier, inc=1, device_id=device)
    for j in range(groups):
        pl.semaphore_signal(barrier, inc=1, device_id={"strip": ring.below, "grp": j})
    loaded()
    for h in blocks:
        rows = pl.ds(h * LANES, LANES)
        for c in range(2):
            column = jnp.broadcast_to(anchor_ref[c : c + 1, h * LANES : (h + 1) * LANES], (LANES, LANES)).T
            state_ref[c, rows, :] = offset_ref[rows, c, :] + column
        state_ref[2, rows, :] = gamma_ref[rows, :]
    pl.semaphore_wait(barrier, 3 + groups)
    rings.first()
    sort_lists(ints_ref, outbox)
    mail = []
    for j in range(groups):
        peer = lax.rem(ring.grp + j, groups)
        copy = pltpu.make_async_remote_copy(
            src_ref=outbox.at[peer],
            dst_ref=lists_ref.at[ring.grp],
            send_sem=list_send.at[j],
            recv_sem=list_recv.at[j],
            device_id={"strip": ring.above, "grp": peer},
        )
        copy.start()
        mail.append(copy)

    for h in blocks:
        rows = pl.ds(h * LANES, LANES)
        for c in range(3):
            turned[h, c] = state_ref[c, rows, :].T
    views = lambda ref, h, n: [ref.at[h, c] for c in range(n)]
    for h in blocks:
        one_sided_lanes(views(turned, h, 2), views(turned, h, 3), views(vel_ref, h, 2))
        rings.rings[h].second()
    first = ints_ref[0:1, :]
    hot_a = places(first)
    hot_b = places(jnp.bitwise_and(first + ints_ref[2:3, :], leaves - 1))
    for c in range(3):
        whole = jnp.concatenate([turned[h, c] for h in blocks], axis=1)
        for ref, hot in ((pa, hot_a), (pb, hot_b)):
            picked = pick_columns(whole, hot)
            for h in blocks:
                ref[h, c] = picked[:, h * LANES : (h + 1) * LANES]
    for h in blocks:
        between = rings.third if h == 0 else lambda: None
        mutual_lanes(views(pa, h, 3), views(pb, h, 3), views(oa, h, 2), views(ob, h, 2), between)
    for c, sign in ((0, -biot_factor), (1, biot_factor)):
        on_a, on_b = [jnp.concatenate([ref[h, c] for h in blocks], axis=1) for ref in (oa, ob)]
        pairs = spread_columns(on_a, hot_a) - spread_columns(on_b, hot_b)
        for h in blocks:
            vel_ref[h, c] = (vel_ref[h, c] + pairs[:, h * LANES : (h + 1) * LANES]) * sign
    rings.finish()
    for copy in mail:
        copy.wait()


def walk(ints_ref, lists_ref, leaves, step, visit):
    live = ints_ref[8 + step, 0]
    shift = leaves.bit_length() - 1

    def mine(k):
        source = ints_ref[6 + step, k]
        block, row = lax.shift_right_logical(source, shift), jnp.bitwise_and(source, leaves - 1)
        visit(k, jnp.where(k < live, ints_ref[4 + step, k], leaves), 0, block, row)

    loop8(live, mine)
    base = live
    for g in range(lists_ref.shape[0]):
        count = lists_ref[g, 4 + step, 0]

        def theirs(k, g=g, base=base, count=count):
            leaf = jnp.where(k < count, lists_ref[g, 2 * step + 1, k], leaves)
            visit(base + k, leaf, 1, g, lists_ref[g, 2 * step, k])

        loop8(count, theirs)
        base = base + count
    return base


def cross_kernel(state_ref, up_ref, down_ref, ints_ref, lists_ref, vel_ref, ra, rb, ta, tb, oa, total_ref):
    leaves = state_ref.shape[1]
    sides = (up_ref, down_ref)
    total_ref[...] = jnp.zeros_like(total_ref)

    def fetch(n, leaf, side, block, row):
        own = jnp.minimum(leaf, leaves - 1)
        for c in range(2):
            ra[c, pl.ds(n, 1), :] = state_ref[c, pl.ds(own, 1), :]
        for c in range(3):
            rb[c, pl.ds(n, 1), :] = sides[side][block, c, pl.ds(row, 1), :]

    total = walk(ints_ref, lists_ref, leaves, 0, fetch)

    def pair_group(i, carry):
        rows = pl.ds(pl.multiple_of(i * LANES, LANES), LANES)
        half = LANES // 2
        few = total - i * LANES <= half

        @pl.when(few)
        def _():
            low = pl.ds(pl.multiple_of(i * LANES, LANES), half)
            high = pl.ds(pl.multiple_of(i * LANES + half, half), half)
            for c in range(2):
                ra[c, high, :] = ra[c, low, :]
            for c in range(3):
                rb[c, high, :] = pltpu.roll(rb[c, low, :], half, 1)

        for c in range(2):
            ta[c] = ra[c, rows, :].T
        for c in range(3):
            tb[c] = rb[c, rows, :].T
        views = [[ref.at[c] for c in range(n)] for ref, n in ((ta, 2), (tb, 3), (oa, 2))]

        @pl.when(few)
        def _():
            one_sided_lanes(*views, 1)

        @pl.when(jnp.logical_not(few))
        def _():
            one_sided_lanes(*views)

        for c, sign in ((0, -biot_factor), (1, biot_factor)):
            found = oa[c].T * sign
            ra[c, rows, :] = found
            ra[c, pl.ds(pl.multiple_of(i * LANES, LANES), half), :] = found[:half] + jnp.where(few, found[half:], 0.0)
        return carry

    lax.fori_loop(0, (total + LANES - 1) // LANES, pair_group, 0)

    def spread(n, leaf, side, block, row):
        for c in range(2):
            total_ref[c, pl.ds(leaf, 1), :] += ra[c, pl.ds(n, 1), :]

    walk(ints_ref, lists_ref, leaves, 0, spread)
    for c in range(2):
        vel_ref[c] = total_ref[c, pl.ds(0, leaves), :]


def lattice_waves(x, y, lat, fwd):
    n = x.shape[0]
    x = jnp.concatenate([x] * 4, axis=1) + lat[0:1, :]
    y = jnp.concatenate([y] * 4, axis=1) + lat[1:2, :]
    w = biot_factor * recip(x * x + y * y + 1.0)
    waves = dot3(jnp.concatenate([-y * w, x * w], axis=0), fwd[0], fwd[1])
    return waves[:n], waves[n:]


def wave_product(k, g, sign):
    kr, ki, gr, gi = k[:, :256], k[:, 256:], g[:, :256], g[:, 256:]
    if sign < 0:
        return jnp.concatenate([kr * gr + ki * gi, kr * gi - ki * gr], axis=1)
    return jnp.concatenate([kr * gr - ki * gi, kr * gi + ki * gr], axis=1)


def load_tables(pairs, sem):
    copies = [pltpu.make_async_copy(src, dst, sem.at[i]) for i, (src, dst) in enumerate(pairs)]
    for copy in copies:
        copy.start()

    def wait():
        for copy in copies:
            copy.wait()

    return wait


def spread_anchors(anchor_ref, half):
    cols = slice(half * LANES, (half + 1) * LANES)
    part = [jnp.broadcast_to(anchor_ref[c : c + 1, cols], (LANES // 4, LANES)) for c in range(2)]
    return jnp.concatenate(part + part, axis=0).T


def cross_waves(
    spread_ref,
    up_ref,
    down_ref,
    vel_in_ref,
    ints_ref,
    lists_ref,
    fwd_in,
    gam_in,
    inv_in,
    lat,
    vel_ref,
    rb,
    rd,
    ra,
    total_ref,
    far_anc,
    fwd,
    gam,
    inv,
    sem,
):
    leaves = vel_in_ref.shape[1]
    sides = (up_ref, down_ref)
    ready = load_tables([(fwd_in, fwd), (gam_in, gam), (inv_in, inv)], sem)
    quarter = LANES // 4
    for side in range(2):
        for b in range(up_ref.shape[0]):
            lines = [
                jnp.broadcast_to(sides[side][b, leaves + q : leaves + q + 1, :], (quarter, LANES)) for q in range(4)
            ]
            anchors = jnp.concatenate(lines, axis=0).T
            far_anc[side, b, pl.ds(0, LANES, stride=2), :] = anchors
            far_anc[side, b, pl.ds(1, LANES, stride=2), :] = pltpu.roll(anchors, LANES // 2, 1)
    for c in range(2):
        total_ref[c, pl.ds(0, leaves), :] = vel_in_ref[c]

    def fetch(n, leaf, side, block, row):
        rb[pl.ds(n, 1), :] = sides[side][block, pl.ds(row, 1), :]
        own = jnp.minimum(leaf, leaves - 1)
        rd[pl.ds(n, 1), :] = spread_ref[pl.ds(own, 1), :] - far_anc[side, block, pl.ds(row, 1), :]

    total = walk(ints_ref, lists_ref, leaves, 1, fetch)
    ready()

    def pair_group(i, carry):
        rows = pl.ds(pl.multiple_of(i * LANES, LANES), LANES)
        waves = dot3(rb[rows, :], gam[0], gam[1])
        gap = rd[rows, :]
        x = jnp.broadcast_to(gap[:, 0:1], (LANES, LANES))
        y = jnp.broadcast_to(gap[:, quarter : quarter + 1], (LANES, LANES))
        products = [wave_product(k, waves, 1) for k in lattice_waves(x, y, lat, fwd)]
        found = dot3(jnp.concatenate(products, axis=0), inv[0], inv[1])
        ra[0, rows, :] = found[:LANES]
        ra[1, rows, :] = found[LANES:]
        return carry

    lax.fori_loop(0, (total + LANES - 1) // LANES, pair_group, 0)

    def spread(n, leaf, side, block, row):
        for c in range(2):
            total_ref[c, pl.ds(leaf, 1), :] += ra[c, pl.ds(n, 1), :]

    walk(ints_ref, lists_ref, leaves, 1, spread)
    for c in range(2):
        vel_ref[c] = total_ref[c, pl.ds(0, leaves), :]


def regroup_kernel(step, *refs):
    last = step == STEPS - 1
    refs = list(refs)
    take = lambda n: [refs.pop(0) for _ in range(n)]
    vel_ref, shift_ref, g_ref, anchor_ref, dest_ref = take(5)
    leaves = vel_ref.shape[1]
    if not last:
        turned_ref, ints_ref, list_ref, fwd_in, gam_in, inv_in, lat, own_in = take(8)
        block, spread_ref, next_vel, up_ref, down_ref = take(5)
    else:
        gamma_ref, final_ref = take(2)
    px, py, pg, wx, out, nodes, outbox, box_ref, send_sem, recv_sem, own_sem = take(11)
    if not last:
        own_ref, ra, rb, rd, fwd, gam, inv, own, ring_send, ring_recv, table_sem = take(11)
        ready = load_tables([(fwd_in, fwd), (gam_in, gam), (inv_in, inv), (own_in, own)], table_sem)
    else:
        (spread_ref,) = take(1)
    if not last:
        part = lambda ref, start, size, *member: ref.at[(*member, pl.ds(start, size))]
        cut = leaves // 2
        chunks = [(0, cut, cut // 2), (cut, cut + 8, cut // 2)]
        rings = Rings(block, own_ref, up_ref, down_ref, part, chunks, ring_send, ring_recv)
        ring = rings.rings[0]
    strip = lax.axis_index("strip")
    strips = outbox.shape[0]
    barrier = pltpu.get_barrier_semaphore()

    def greet(d, carry):
        pl.semaphore_signal(barrier, inc=1, device_id={"strip": jnp.bitwise_and(strip + d, strips - 1)})
        return carry

    lax.fori_loop(1, strips, greet, 0, unroll=8)
    if not last:
        for device in ({"grp": ring.left}, {"grp": ring.right}):
            pl.semaphore_signal(barrier, inc=1, device_id=device)

    def remesh(i, carry):
        rows = pl.ds(pl.multiple_of(i * LANES, LANES), LANES)
        for c, dst in ((0, px), (1, py)):
            if last:
                node = lax.broadcasted_iota(jnp.int32, (LANES, LANES), 0)
                node = jnp.bitwise_and(node, WY - 1) if c else lax.shift_right_logical(node, WY.bit_length() - 1)
                dst[...] = node.astype(f32) + (time_step * vel_ref[c, rows, :]).T
            else:
                moved = (shift_ref[rows, c, :] + time_step * vel_ref[c, rows, :]).T
                dst[...] = moved + time_step * turned_ref[i, c]
        pg[...] = g_ref[rows, :].T
        remesh_lanes(px, py, pg, wx, out)
        nodes[rows, :] = out[...].T
        return carry

    lax.fori_loop(0, leaves // LANES, remesh, 0)
    dest = dest_ref[step]
    named = jnp.where(lax.broadcasted_iota(jnp.int32, (strips, leaves), 0) == dest, 1.0, 0.0)
    rank = jnp.sum(named * dot(named.astype(bf16), earlier(leaves)), axis=0, keepdims=True)
    hot = [onehot(jnp.where(rank == float(r), named, 0.0) > 0.5) for r in range(2)]
    for r in range(2):
        outbox[:, r, :] = dot_exact(hot[r], nodes[...])
    lane = lax.broadcasted_iota(jnp.int32, (strips, LANES), 1)
    if last:
        spread = anchor_ref[...]
    else:
        spread = jnp.concatenate([spread_anchors(anchor_ref, h) for h in range(leaves // LANES)], axis=0)
    anchors = [dot_exact(hot[r], spread) for r in range(2)]
    outbox[:, 2, :] = jnp.where(lane < LANES // 2, anchors[0], anchors[1])
    pl.semaphore_wait(barrier, strips - 1 + (0 if last else 2))

    def send(d, carry):
        to = jnp.bitwise_and(strip + d, strips - 1)
        pltpu.make_async_remote_copy(
            src_ref=outbox.at[to],
            dst_ref=box_ref.at[strip],
            send_sem=send_sem,
            recv_sem=recv_sem,
            device_id={"strip": to},
        ).start()
        return carry

    lax.fori_loop(1, strips, send, 0, unroll=8)
    mine = pltpu.make_async_copy(outbox.at[strip], box_ref.at[strip], own_sem)
    mine.start()
    mine.wait()
    rest = pl.ds(0, strips - 1)
    pltpu.make_async_copy(box_ref.at[rest], box_ref.at[rest], recv_sem).wait()
    pltpu.make_async_copy(outbox.at[rest], outbox.at[rest], send_sem).wait()
    anchors = box_ref[:, 2, :]
    rolled = pltpu.roll(anchors, LANES // 2, 1)
    if last:
        for r in range(2):
            gamma_ref[pl.ds(r, strips, stride=2), :] = box_ref[:, r, :]
        spread_ref[pl.ds(0, strips, stride=2), :] = anchors
        spread_ref[pl.ds(1, strips, stride=2), :] = rolled
        for h in range(leaves // LANES):
            turned = spread_ref[pl.ds(h * LANES, LANES), :].T
            for c in range(2):
                row = turned[c * (LANES // 4) : c * (LANES // 4) + 1, :]
                final_ref[c : c + 1, h * LANES : (h + 1) * LANES] = row
        return
    for r in range(2):
        block[pl.ds(r, strips, stride=2), :] = box_ref[:, r, :]
    turned = anchors.T
    for q in range(4):
        block[leaves + q : leaves + q + 1, :] = turned[q * (LANES // 4) : q * (LANES // 4) + 1, :]
    block[leaves + 4 : leaves + 8, :] = jnp.zeros((4, LANES), f32)
    rings.first()
    spread_ref[pl.ds(0, strips, stride=2), :] = jnp.where(lane < LANES // 2, anchors, rolled)
    spread_ref[pl.ds(1, strips, stride=2), :] = jnp.where(lane < LANES // 2, rolled, anchors)
    ready()
    field = dot3(block[pl.ds(0, leaves), :], own[0], own[1])

    def pair_group(i, between):
        base = i * LANES

        def fetch(k):
            start = list_ref[1, base + k]
            first = pl.ds(start, 1)
            second = pl.ds(jnp.bitwise_and(start + list_ref[3, base + k], leaves - 1), 1)
            row = pl.ds(base + k, 1)
            ra[0, row, :] = block[first, :]
            rb[0, row, :] = block[second, :]
            rd[row, :] = spread_ref[first, :] - spread_ref[second, :]

        loop8(LANES, fetch)
        between()
        rows = pl.ds(base, LANES)
        gap = rd[rows, :]
        x = jnp.broadcast_to(gap[:, 0:1], (LANES, LANES))
        y = jnp.broadcast_to(gap[:, LANES // 4 : LANES // 4 + 1], (LANES, LANES))
        waves = dot3(jnp.concatenate([ra[0, rows, :], rb[0, rows, :]], axis=0), gam[0], gam[1])
        wa, wb = waves[:LANES], waves[LANES:]
        kernels = lattice_waves(x, y, lat, fwd)
        products = [wave_product(k, wb, 1) for k in kernels] + [wave_product(k, wa, -1) for k in kernels]
        found = dot3(jnp.concatenate(products, axis=0), inv[0], inv[1])
        for c in range(2):
            ra[c, rows, :] = found[c * LANES : (c + 1) * LANES]
            rb[c, rows, :] = found[(2 + c) * LANES : (3 + c) * LANES]

    for i in range(leaves // LANES):
        pair_group(i, (rings.second, rings.third)[i] if i < 2 else lambda: None)
    first = ints_ref[1:2, :]
    second = jnp.bitwise_and(first + ints_ref[3:4, :], leaves - 1)
    for c in range(2):
        next_vel[c] = (
            field[:, c * LANES : (c + 1) * LANES]
            + spread_rows(first, ra[c])
            - spread_rows(second, rb[c])
        )
    rings.finish()


def shape(*sizes, dtype=f32):
    return jax.ShapeDtypeStruct(sizes, dtype)


def anywhere():
    return pl.BlockSpec(memory_space=pl.ANY)


def call(kernel, out_shape, in_specs, out_specs, scratch, vmem=48, **kw):
    return pl.pallas_call(
        kernel,
        out_shape=out_shape,
        in_specs=in_specs,
        out_specs=out_specs,
        scratch_shapes=scratch,
        compiler_params=pltpu.CompilerParams(vmem_limit_bytes=vmem * 2**20, **kw),
    )


def run_local(offsets, gamma, anchor, ints):
    leaves = gamma.shape[0]
    groups = lax.axis_size("grp")
    state = (3, leaves, LANES)
    wide = (groups,) + state
    dma = pltpu.SemaphoreType.DMA
    cols = lambda n: pltpu.VMEM((leaves // LANES, n, LANES, LANES), f32)
    return call(
        local_kernel,
        (shape(*state), shape(leaves // LANES, 2, LANES, LANES), shape(groups, 8, leaves, dtype=jnp.int32)) + (shape(*wide),) * 3,
        [pl.BlockSpec(memory_space=pltpu.HBM)] * 3 + [vspec()],
        (vspec(),) * 3 + (anywhere(),) * 3,
        [pltpu.VMEM(offsets.shape, f32), pltpu.VMEM(gamma.shape, f32), pltpu.VMEM(anchor.shape, f32)]
        + [pltpu.VMEM((groups, 8, leaves), jnp.int32), cols(3), cols(3), cols(3), cols(2), cols(2)]
        + [dma((3,)), dma((2, 12)), dma((2, 12)), dma((groups,)), dma((groups,))],
        collective_id=0,
        has_side_effects=True,
    )(offsets, gamma, anchor, ints)[:5]


def run_cross(state, up, down, ints, lists):
    leaves = state.shape[1]
    most = (1 + up.shape[0]) * leaves + LANES
    return call(
        cross_kernel,
        shape(2, leaves, LANES),
        [vspec()] * 3 + [sspec()] * 2,
        vspec(),
        [pltpu.VMEM((2, most, LANES), f32), pltpu.VMEM((3, most, LANES), f32), tiles(2), tiles(3), tiles(2)]
        + [pltpu.VMEM((2, leaves + 8, LANES), f32)],
    )(state, up, down, ints, lists)


def run_cross_waves(spread, up, down, vel, ints, lists, tables):
    leaves = vel.shape[1]
    groups = up.shape[0]
    most = (1 + groups) * leaves + 8
    fwd, gam, inv, lat, own = tables
    return call(
        cross_waves,
        shape(*vel.shape),
        [vspec()] * 4 + [sspec()] * 2 + [anywhere()] * 3 + [vspec()],
        vspec(),
        [pltpu.VMEM((most, LANES), f32), pltpu.VMEM((most, LANES), f32), pltpu.VMEM((2, most, LANES), f32)]
        + [pltpu.VMEM((2, leaves + 8, LANES), f32), pltpu.VMEM((2, groups, leaves, LANES), f32)]
        + [pltpu.VMEM(t.shape, bf16) for t in (fwd, gam, inv)]
        + [pltpu.SemaphoreType.DMA((3,))],
    )(spread, up, down, vel, ints, lists, fwd, gam, inv, lat)


def run_regroup(step, vel, shifted, gamma, anchor, dest, *more):
    last = step == STEPS - 1
    leaves = vel.shape[1]
    groups, strips = lax.axis_size("grp"), lax.axis_size("strip")
    dma = pltpu.SemaphoreType.DMA
    box = (strips, 3, LANES)
    in_specs = [vspec()] * 5
    scratch = [tile(), tile(), tile(), pltpu.VMEM((4, WX, LANES), f32), tile(), pltpu.VMEM((leaves, LANES), f32)]
    scratch += [pltpu.VMEM(box, f32), pltpu.VMEM(box, f32), dma, dma, dma]
    if last:
        out_shape = [shape(leaves, LANES), shape(2, leaves)]
        scratch += [pltpu.VMEM((leaves, LANES), f32)]
    else:
        block = (leaves + 8, LANES)
        wide = (groups,) + block
        out_shape = [shape(*block), shape(leaves, LANES), shape(2, leaves, LANES), shape(*wide), shape(*wide)]
        in_specs += [vspec(), vspec(), sspec()] + [anywhere()] * 3 + [vspec(), anywhere()]
        rows = lambda n: pltpu.VMEM((n, leaves, LANES), f32)
        scratch += [pltpu.VMEM(wide, f32), rows(2), rows(2), pltpu.VMEM((leaves, LANES), f32)]
        scratch += [pltpu.VMEM(more[i].shape, bf16) for i in (3, 4, 5, 7)]
        scratch += [dma((2, 12)), dma((2, 12)), dma((4,))]
    return call(
        functools.partial(regroup_kernel, step),
        tuple(out_shape),
        in_specs,
        (vspec(),) * len(out_shape),
        scratch,
        collective_id=1 + step,
        has_side_effects=True,
    )(vel, shifted, gamma, anchor, dest, *more)


def on_device(
    offsets,
    circulation,
    window_anchor,
    local_first,
    local_offset,
    cross_target,
    cross_source,
    cross_count,
    destination,
):
    anchor = window_anchor.T
    dest = destination.transpose(0, 2, 1)
    live = jnp.broadcast_to(cross_count, local_first.shape)
    ints = jnp.concatenate([local_first, local_offset, cross_target, cross_source, live, live, live, live], axis=0)
    tables = [jnp.asarray(t) for t in fourier_tables()]
    state, turned, inbox, up, down = run_local(offsets, circulation, anchor, ints)
    vel = run_cross(state, up, down, ints, inbox)
    block, spread, vel, up, down = run_regroup(
        0, vel, offsets, circulation, anchor, dest, turned, ints, ints, *tables
    )
    vel = run_cross_waves(spread, up, down, vel, ints, inbox, tables)
    gamma, anchor = run_regroup(1, vel, block, block, spread, dest)
    return gamma, anchor.T


def solution(mesh):
    rows = P(("strip", "grp"))
    lists = P(None, ("strip", "grp"))
    return jax.shard_map(
        on_device,
        mesh=mesh,
        in_specs=(rows, rows, rows, lists, lists, lists, lists, lists, lists),
        out_specs=(rows, rows),
        check_vma=False,
    )
```
